256 devices in a mesh: ctx: 8 (over y_lo, x), zero: 32 (over z, y_hi, core).
Axes of the slice: x: 4, y: 4 (y_hi: 2, y_lo: 2; y = y_hi * 2 + y_lo), z: 8, core: 2. Of those that a mesh axis runs over, the one named last changes fastest.
Arguments:
- tokens: bfloat16 [4, 2048, 8192], P(None, 'ctx', 'zero'), may hold values from -48 to 48
- q_weight: bfloat16 [8192, 4096], P('zero'), may hold values from -0.0625 to 0.0625
- forget_weight: bfloat16 [8192, 4096], P('zero'), may hold values from -0.0625 to 0.0625
- value_weight: bfloat16 [8192, 4096], P('zero'), may hold values from -0.0625 to 0.0625
- forget_bias: float32 [4096], P('zero'), may hold values from 3 to 16
- norm_gain: float32 [4096], P('zero'), may hold values from 0.1 to 1.9
Outputs:
- head_out: bfloat16 [4, 2048, 4096], P(None, 'ctx', 'zero')
The draws below stay inside these ranges and needn't reach their ends.
All inputs are finite; a program needn't handle non-finite values.
Results may differ from the reference program's by a relative error of at most 0.0015.
Values may be sent and summed in bfloat16 or wider, within the bound.
A program may use at most 128 MiB of HBM per device.

```python
import jax
import jax.numpy as jnp
from jax import lax

D = 8192
HEADS = 32
HEAD = 128
BLK = 64
SEQUENCE_COUNT = 4
SEQUENCE_LENGTH = 2048
HIDDEN_UNITS = 4096


def draw_tokens(key, part):
    key = jax.random.fold_in(key, 11)
    key_baseline, key_spike = jax.random.split(key, 2)
    spike_amplitude = jax.random.uniform(key_spike, (SEQUENCE_COUNT, SEQUENCE_LENGTH, 1)) < 4.0 / SEQUENCE_LENGTH
    scale_multiplier = jnp.where(spike_amplitude, 8.0, 1.0)
    base = jnp.clip(jax.random.normal(key_baseline, (SEQUENCE_COUNT, SEQUENCE_LENGTH, D)), -5.5, 5.5)
    values = base * scale_multiplier
    return values.astype(jnp.bfloat16)


def draw_forget_bias(key, part):
    key = jax.random.fold_in(key, 23)
    key_pick, key_slow, key_fast = jax.random.split(key, 3)
    count = HEADS * HEAD
    slow = jax.random.uniform(key_pick, (count,)) < 0.5
    slow_rate = jnp.exp(jax.random.uniform(key_slow, (count,), minval=jnp.log(0.3), maxval=jnp.log(2.0))) / SEQUENCE_LENGTH
    fast_rate = jnp.exp(jax.random.uniform(key_fast, (count,), minval=jnp.log(1.0 / 50.0), maxval=jnp.log(1.0 / 25.0)))
    rate = jnp.where(slow, slow_rate, fast_rate)
    return (-jnp.log(rate) + 0.5).astype(jnp.float32)


def steps_of(key, extent, cuts, smallest, high):
    loudness = 1.0
    for dim, shards_of in cuts:
        draws = jax.random.uniform(jax.random.fold_in(jax.random.fold_in(key, 6), dim), (shards_of,), jnp.float32, smallest / len(cuts), high / len(cuts))
        loudness = loudness * jnp.repeat(jnp.exp(draws), extent[dim] // shards_of).reshape((-1,) + (1,) * (len(extent) - 1 - dim))
    return loudness


def gaussian(rng, extent, width, limit, shards=(), held_as=jnp.bfloat16):
    array = width * jax.random.normal(rng, extent, jnp.float32)
    if shards:
        array = array * steps_of(rng, extent, shards, -0.22, 0.18)
    return jnp.clip(array, -limit, limit).astype(held_as)


def setup_inputs(seed: int = 0) -> dict:
    streams_of = jax.random.split(jax.random.key(seed), 7)
    tokens = draw_tokens(jax.random.fold_in(streams_of[6], 71), 0)
    q_weight = gaussian(streams_of[1], (D, HIDDEN_UNITS), D ** -0.5, 0.0625, ((0, 32),))
    forget_weight = gaussian(streams_of[2], (D, HIDDEN_UNITS), D ** -0.5, 0.0625, ((0, 32),))
    value_weight = gaussian(streams_of[3], (D, HIDDEN_UNITS), D ** -0.5, 0.0625, ((0, 32),))
    forget_bias = draw_forget_bias(jax.random.fold_in(streams_of[6], 71), 0)
    norm_gain = jnp.clip(1.0 + 0.18 * jax.random.normal(streams_of[5], (HIDDEN_UNITS,), jnp.float32), 0.1, 1.9)
    return {"tokens": tokens, "q_weight": q_weight, "forget_weight": forget_weight, "value_weight": value_weight, "forget_bias": forget_bias, "norm_gain": norm_gain}


def block_step(carried, block):
    queries, log_forget, in_gate, values = block
    cum_log = jnp.cumsum(log_forget, axis=0)
    log_gap = cum_log[:, None, :] - cum_log[None, :, :]
    positions = jnp.arange(queries.shape[0], dtype=jnp.int32)
    causal = (positions[:, None] >= positions[None, :])[:, :, None]
    decays = jnp.where(causal, jnp.exp(jnp.minimum(log_gap, 0.0)), 0.0)
    scores = jnp.einsum('tc,sc,tsc->ts', queries, in_gate, decays, precision=lax.Precision.HIGHEST)
    within = jnp.dot(scores, values, precision=lax.Precision.HIGHEST)
    from_state = jnp.dot(queries * jnp.exp(cum_log), carried, precision=lax.Precision.HIGHEST)
    to_end = jnp.exp(cum_log[-1:] - cum_log)
    updated = jnp.exp(cum_log[-1])[:, None] * carried + jnp.dot((in_gate * to_end).T, values, precision=lax.Precision.HIGHEST)
    return (updated, within + from_state)

def scan_blocks(queries, log_forget, in_gate, values):
    block_count = queries.shape[0] // BLK
    shaped = tuple((item.reshape(block_count, BLK, item.shape[1]) for item in (queries, log_forget, in_gate, values)))
    start_state = jnp.zeros((queries.shape[1], values.shape[1]), jnp.float32)
    final_state, outputs = lax.scan(block_step, start_state, shaped)
    return (outputs.reshape(queries.shape), final_state)

def reference(tokens, q_weight, forget_weight, value_weight, forget_bias, norm_gain):
    gains = norm_gain.reshape(HEADS, HEAD)

    def one_sequence(rows_in):
        length = rows_in.shape[0]
        queries = jnp.dot(rows_in, q_weight, preferred_element_type=jnp.float32)
        logit = jnp.dot(rows_in, forget_weight, preferred_element_type=jnp.float32) + forget_bias
        values = jnp.dot(rows_in, value_weight, preferred_element_type=jnp.float32)
        log_forget = jax.nn.log_sigmoid(logit)
        in_gate = jax.nn.sigmoid(-logit)

        def split(item):
            return item.reshape(length, HEADS, HEAD).transpose(1, 0, 2)

        def one_head(items):
            head_q, head_lf, head_ig, head_v, head_gain = items
            outputs, final_state = scan_blocks(head_q, head_lf, head_ig, head_v)
            mean_square = lax.optimization_barrier(jnp.mean(outputs * outputs, axis=-1, keepdims=True))
            return (outputs * lax.rsqrt(mean_square + 1e-05) * head_gain).astype(jnp.bfloat16)
        normed = lax.map(one_head, (split(queries), split(log_forget), split(in_gate), split(values), gains))
        return normed.transpose(1, 0, 2).reshape(length, HEADS * HEAD)
    return lax.map(one_sequence, tokens)
```

```python
import functools

import jax
import jax.numpy as jnp
import numpy as np
from jax import lax
from jax.experimental import pallas as pl
from jax.experimental.pallas import tpu as pltpu
from jax.sharding import PartitionSpec as P

MESH = pl.DeviceIdType.MESH
HEAD = 128
TILE = 128
LEVELS = (64, 32, 16, 8, 4, 2, 1)
OFFSETS = (0, 1, 7, 2, 6, 3, 5, 4)
SLOT = {offset: i for i, offset in enumerate(OFFSETS)}
X, Z = 4, 8


def coords():
    c, zi = lax.axis_index("ctx"), lax.axis_index("zero")
    return lax.rem(c, X), c // X, zi // 4, lax.rem(zi // 2, 2), lax.rem(zi, 2)


def place(x, yl, z, yh, k):
    return (yl * X + x, z * 4 + yh * 2 + k)


def wrap(value, n):
    return lax.rem(value + n, n)


def gather_kernel(tok, wq, wf, wv, proj, w_all, t_all, acc, other, local_sem, w1_s, w1_r, w2_s, w2_r, w3_s, w3_r, w4_s, w4_r,
                  y0_s, y0_r, y1_s, y1_r, z_s, z_r, z2_s, p_s, p_r):
    x, yl, z, yh, k = coords()
    seqs = t_all.shape[0]
    started = []

    def send(src, dst, ss, rs, target):
        copy = pltpu.make_async_remote_copy(src, dst, ss, rs, device_id=target, device_id_type=MESH)
        copy.start()
        started.append(copy)
        return copy

    z_next, z_prev = wrap(z + 1, Z), wrap(z - 1, Z)
    x_next, x_prev = wrap(x + 1, X), wrap(x - 1, X)
    up = place(x, yl, z_next, yh, k)
    down = place(x, yl, z_prev, yh, k)
    right = place(x_next, yl, z, yh, k)
    left = place(x_prev, yl, z, yh, k)
    far = place(x, yl, z, 1 - yh, k)
    pair = place(x, 1 - yl, z, yh, k)
    sibling = place(x, yl, z, yh, 1 - k)

    barrier = pltpu.get_barrier_semaphore()
    peers = [right, left, pair, sibling]
    for dz in range(Z):
        for dy in range(2):
            if dz or dy:
                peers.append(place(x, yl, wrap(z + dz, Z), 1 - yh if dy else yh, k))
    for peer in peers:
        pl.semaphore_signal(barrier, inc=1, device_id=peer, device_id_type=MESH)
    pl.semaphore_wait(barrier, len(peers))

    own = pltpu.make_async_copy(tok, t_all.at[:, 0, pl.ds(0, 256)], local_sem.at[0])
    own.start()
    y0 = [send(tok.at[s, pl.ds(0, 128)], t_all.at[s, 0, pl.ds(256, 128)], y0_s.at[s], y0_r.at[s], far) for s in range(seqs)]

    part = pl.multiple_of((x * 2 + yl) * 32, 32)
    w1 = {}
    locals_ = []
    for i, dz in enumerate(OFFSETS):
        for dy in range(2):
            zt, yt = wrap(z - dz, Z), 1 - yh if dy else yh
            cols = pl.multiple_of((zt * 2 + yt) * 256, 256)
            for w, ref in enumerate((wq, wf, wv)):
                src = ref.at[pl.ds(part, 32), pl.ds(cols, 256)]
                dst = w_all.at[2 * i + dy, pl.ds(part, 32), pl.ds(w * 256, 256)]
                if i == 0 and dy == 0:
                    copy = pltpu.make_async_copy(src, dst, local_sem.at[1 + w])
                    copy.start()
                    locals_.append(copy)
                else:
                    w1[2 * i + dy, w] = send(src, dst, w1_s.at[2 * i + dy, w], w1_r.at[2 * i + dy, w], place(x, yl, zt, yt, k))
    y1 = {}
    for s in range(seqs):
        y1[s, 0] = send(tok.at[s, pl.ds(128, 128)], t_all.at[s, 0, pl.ds(384, 128)], y1_s.at[s, 0], y1_r.at[s, 0], far)
    own.wait()

    zc = {}

    def ring_start(s):
        y0[s].wait_recv()
        block = t_all.at[s, 0, pl.ds(0, 384)]
        zc[s, SLOT[7]] = send(block, t_all.at[s, SLOT[7], pl.ds(0, 384)], z_s.at[s, SLOT[7]], z_r.at[s, SLOT[7]], up)
        zc[s, SLOT[1]] = send(block, t_all.at[s, SLOT[1], pl.ds(0, 384)], z_s.at[s, SLOT[1]], z_r.at[s, SLOT[1]], down)

    def ring_hop(s, h):
        for sign, target in ((-1, up), (1, down)):
            last = 4 if (sign < 0) == (s % 2 == 0) else 3
            if h > last:
                continue
            here, there = SLOT[sign * h % Z], SLOT[sign * (h + 1) % Z]
            zc[s, here].wait_recv()
            if h < last:
                zc[s, there] = send(t_all.at[s, here, pl.ds(0, 384)], t_all.at[s, there, pl.ds(0, 384)],
                                    z_s.at[s, there], z_r.at[s, there], target)
            y1[s, here] = send(t_all.at[s, here, pl.ds(128, 128)], t_all.at[s, here, pl.ds(384, 128)],
                               y1_s.at[s, here], y1_r.at[s, here], far)

    w2, w3, w4 = {}, {}, {}

    def weights_1(g):
        if g == 0:
            for copy in locals_:
                copy.wait()
        for slot in range(4 * g, 4 * g + 4):
            if slot:
                for w in range(3):
                    w1[slot, w].wait_recv()
        piece = w_all.at[pl.ds(4 * g, 4), pl.ds(part, 32)]
        w2[g] = send(piece, piece, w2_s.at[g], w2_r.at[g], pair)

    def rows_of(g, xx):
        return w_all.at[pl.ds(4 * g, 4), pl.ds(pl.multiple_of(xx * 64, 64), 64)]

    def weights_2(g):
        w2[g].wait_recv()
        piece = rows_of(g, x)
        w3[0, g] = send(piece, piece, w3_s.at[0, g], w3_r.at[0, g], right)
        w3[1, g] = send(piece, piece, w3_s.at[1, g], w3_r.at[1, g], left)

    def weights_3(g):
        w3[0, g].wait_recv()
        w3[1, g].wait_recv()
        if g % 2 == 0:
            piece = rows_of(g, x_prev)
            w4[g] = send(piece, piece, w4_s.at[g], w4_r.at[g], right)
        else:
            piece = rows_of(g, x_next)
            w4[g] = send(piece, piece, w4_s.at[g], w4_r.at[g], left)

    pc = {}

    def project(s):
        if s == 0:
            for g in range(4):
                w4[g].wait_recv()
        for i in range(Z):
            y1[s, i].wait_recv()
        lhs = jnp.concatenate([t_all[s, i, pl.ds(dy * 256, 256), :] for i in range(Z) for dy in range(2)], axis=1)
        for n in range(3):
            rhs = w_all[:, :, pl.ds(n * 256, 256)].reshape(16 * 256, 256)
            acc[s, :, pl.ds(n * 256, 256)] = jnp.dot(lhs, rhs, preferred_element_type=jnp.float32)
        theirs = pl.multiple_of((1 - k) * 128, 128)
        for n in range(3):
            pc[s, n] = send(acc.at[s, :, pl.ds(n * 256 + theirs, 128)], other.at[s, :, pl.ds(n * 128, 128)],
                            p_s.at[s, n], p_r.at[s, n], sibling)

    def collect(s):
        mine = pl.multiple_of(k * 128, 128)
        for n in range(3):
            pc[s, n].wait_recv()
            proj[s, :, pl.ds(n * 128, 128)] = acc[s, :, pl.ds(n * 256 + mine, 128)] + other[s, :, pl.ds(n * 128, 128)]

    ring_start(0)
    ring_start(1)
    weights_1(0)
    weights_1(1)
    ring_hop(0, 1)
    ring_hop(1, 1)
    weights_1(2)
    weights_1(3)
    weights_2(0)
    weights_2(1)
    ring_hop(0, 2)
    ring_hop(1, 2)
    weights_2(2)
    weights_2(3)
    ring_start(2)
    ring_hop(0, 3)
    ring_hop(1, 3)
    ring_start(3)
    weights_3(0)
    weights_3(1)
    ring_hop(0, 4)
    ring_hop(1, 4)
    ring_hop(2, 1)
    ring_hop(3, 1)
    weights_3(2)
    weights_3(3)
    ring_hop(2, 2)
    ring_hop(3, 2)
    project(0)
    ring_hop(2, 3)
    ring_hop(3, 3)
    project(1)
    ring_hop(2, 4)
    ring_hop(3, 4)
    collect(0)
    collect(1)
    project(2)
    project(3)
    collect(2)
    collect(3)
    for copy in started:
        copy.wait_send()


def gather_project(tokens, q_weight, forget_weight, value_weight):
    seqs = tokens.shape[0]
    dma = pltpu.SemaphoreType.DMA
    any_ = pl.BlockSpec(memory_space=pl.ANY)
    return pl.pallas_call(
        gather_kernel,
        out_shape=jax.ShapeDtypeStruct((seqs, 256, 384), jnp.float32),
        in_specs=[any_] * 4,
        out_specs=pl.BlockSpec(memory_space=pltpu.VMEM),
        scratch_shapes=[
            pltpu.VMEM((16, 256, 768), jnp.bfloat16),
            pltpu.VMEM((seqs, Z, 512, 256), jnp.bfloat16),
            pltpu.VMEM((seqs, 256, 768), jnp.float32),
            pltpu.VMEM((seqs, 256, 384), jnp.float32),
            dma((4,)),
            dma((16, 3)), dma((16, 3)),
            dma((4,)), dma((4,)),
            dma((2, 4)), dma((2, 4)),
            dma((4,)), dma((4,)),
            dma((seqs,)), dma((seqs,)),
            dma((seqs, Z)), dma((seqs, Z)),
            dma((seqs, Z)), dma((seqs, Z)),
            dma((1,)),
            dma((seqs, 3)), dma((seqs, 3)),
        ],
        compiler_params=pltpu.CompilerParams(collective_id=0, has_side_effects=True, vmem_limit_bytes=56 * 2**20),
        name="gather_project",
    )(tokens, q_weight, forget_weight, value_weight)


def decay_sums():
    t = np.arange(TILE)[:, None]
    r = np.arange(TILE)[None, :]
    rows = []
    for m in LEVELS:
        start = t // m * m
        upper = (t // m) % 2 == 1
        rows.append(np.where(upper, (r >= start) & (r <= t), (r > t) & (r < start + m)))
    rows.append(r <= t)
    rows.append(r > t)
    one = np.concatenate(rows, axis=0)
    return np.concatenate([one, one, one], axis=1).astype(np.float32)


def halves(value):
    high = value.astype(jnp.bfloat16)
    return high, (value - high.astype(jnp.float32)).astype(jnp.bfloat16)


def dot3(a, b, contract):
    (ah, al), (bh, bl) = a, b
    lhs = jnp.concatenate([ah, ah, al], axis=contract[0])
    rhs = jnp.concatenate([bh, bl, bh], axis=contract[1])
    return lax.dot_general(lhs, rhs, (((contract[0],), (contract[1],)), ((), ())), preferred_element_type=jnp.float32)


def log1p_unit(e):
    w = e / (2.0 + e)
    w2 = w * w
    series = jnp.full_like(w2, 1.0 / 17)
    for odd in (15, 13, 11, 9, 7, 5, 3, 1):
        series = series * w2 + 1.0 / odd
    return 2.0 * w * series


def recur_kernel(proj, bias, gain, sums, out, local_out, q_decayed, states, total, from_pair, xs_s, xs_r, ys_s, ys_r):
    x, yl, z, yh, k = coords()
    seqs = proj.shape[0]
    pair = place(x, 1 - yl, z, yh, k)
    row = [place(wrap(x + j, X), yl, z, yh, k) for j in (1, 2, 3)]
    barrier = pltpu.get_barrier_semaphore()
    for peer in row + [pair]:
        pl.semaphore_signal(barrier, inc=1, device_id=peer, device_id_type=MESH)
    pl.semaphore_wait(barrier, 4)

    def state_copy(s, j):
        piece = states.at[s, x]
        return pltpu.make_async_remote_copy(piece, piece, xs_s.at[s, j], xs_r.at[s, j], device_id=row[j], device_id_type=MESH)

    def total_copy(s):
        return pltpu.make_async_remote_copy(total.at[s], from_pair.at[s], ys_s.at[s], ys_r.at[s], device_id=pair, device_id_type=MESH)

    t = lax.broadcasted_iota(jnp.int32, (TILE, TILE), 0)
    r = lax.broadcasted_iota(jnp.int32, (TILE, TILE), 1)

    def local(s, _):
        logit = proj[s, :, pl.ds(128, 128)] + bias[...]
        e = jnp.exp(-jnp.abs(logit))
        log_forget = jnp.minimum(logit, 0.0) - log1p_unit(e)
        gate = jnp.where(logit >= 0.0, e, 1.0) / (1.0 + e)
        wide = jnp.concatenate([log_forget[:TILE], log_forget[TILE:]], axis=1)
        high = wide.astype(jnp.bfloat16)
        rest = wide - high.astype(jnp.float32)
        mid = rest.astype(jnp.bfloat16)
        low = (rest - mid.astype(jnp.float32)).astype(jnp.bfloat16)
        stacked = jnp.concatenate([high, mid, low], axis=0)

        def decays(i):
            return jnp.exp(jnp.dot(sums[pl.ds(i * TILE, TILE), :], stacked, preferred_element_type=jnp.float32))

        from_start, to_end = decays(len(LEVELS)), decays(len(LEVELS) + 1)
        queries = [proj[s, pl.ds(u * TILE, TILE), pl.ds(0, 128)] for u in range(2)]
        keys = [gate[u * TILE : (u + 1) * TILE] for u in range(2)]
        scores = [jnp.where(t == r, jnp.sum(queries[u] * keys[u], axis=1, keepdims=True), 0.0) for u in range(2)]
        for i, m in enumerate(LEVELS):
            level = decays(i)
            upper = (t // m) % 2 == 1
            differ = t ^ r
            mask = (differ >= m) & (differ < 2 * m) & (t > r)
            for u in range(2):
                item = halves(jnp.where(upper, queries[u], keys[u]) * level[:, u * 128 : (u + 1) * 128])
                scores[u] = jnp.where(mask, dot3(item, item, (1, 1)), scores[u])
        state, decay = None, None
        for u in range(2):
            lanes = slice(u * 128, (u + 1) * 128)
            values = halves(proj[s, pl.ds(u * TILE, TILE), pl.ds(256, 128)])
            own = dot3(values, halves(keys[u] * to_end[:, lanes]), (0, 0))
            own_decay = from_start[TILE - 1 : TILE, lanes]
            outputs = dot3(halves(scores[u]), values, (1, 0))
            decayed = queries[u] * from_start[:, lanes]
            if u == 0:
                state, decay = own, own_decay
            else:
                outputs = outputs + dot3(halves(decayed), halves(state), (1, 1))
                decayed = decayed * decay
                state, decay = state * own_decay + own, decay * own_decay
            local_out[s, pl.ds(u * TILE, TILE), :] = outputs
            q_decayed[s, pl.ds(u * TILE, TILE), :] = decayed
        states[s, x, pl.ds(0, 128), :] = state
        states[s, x, pl.ds(128, 8), :] = jnp.broadcast_to(decay, (8, 128))
        for j in range(3):
            state_copy(s, j).start()
        return 0

    lax.fori_loop(0, seqs, local, 0)

    def along_x(s, _):
        for j in range(3):
            state_copy(s, j).wait_recv()
        run = jnp.zeros((HEAD, HEAD), jnp.float32)
        run_decay = jnp.ones((1, HEAD), jnp.float32)
        before, before_decay = run, run_decay
        for xx in range(X):
            before = jnp.where(xx == x, run, before)
            before_decay = jnp.where(xx == x, run_decay, before_decay)
            decay = states[s, xx, pl.ds(128, 1), :]
            run = run * decay + states[s, xx, pl.ds(0, 128), :]
            run_decay = run_decay * decay
        total[s] = run
        total_copy(s).start()
        for j in range(3):
            state_copy(s, j).wait_send()
        states[s, x, pl.ds(0, 128), :] = before
        states[s, x, pl.ds(128, 8), :] = jnp.broadcast_to(before_decay, (8, 128))
        return 0

    lax.fori_loop(0, seqs, along_x, 0)

    def finish(s, _):
        total_copy(s).wait_recv()
        incoming = states[s, x, pl.ds(0, 128), :]
        earlier = from_pair[s] * states[s, x, pl.ds(128, 1), :]
        incoming = incoming + jnp.where(yl == 1, earlier, 0.0)
        outputs = local_out[s] + dot3(halves(q_decayed[s]), halves(incoming), (1, 1))
        mean_square = jnp.mean(outputs * outputs, axis=-1, keepdims=True)
        out[s] = (outputs * lax.rsqrt(mean_square + 1e-05) * gain[...]).astype(jnp.bfloat16)
        total_copy(s).wait_send()
        return 0

    lax.fori_loop(0, seqs, finish, 0)


def recur(proj, bias, gain):
    seqs = proj.shape[0]
    dma = pltpu.SemaphoreType.DMA
    vmem = pl.BlockSpec(memory_space=pltpu.VMEM)
    sums = jnp.asarray(decay_sums(), jnp.bfloat16)
    return pl.pallas_call(
        recur_kernel,
        out_shape=jax.ShapeDtypeStruct((seqs, 256, HEAD), jnp.bfloat16),
        in_specs=[vmem] * 4,
        out_specs=vmem,
        scratch_shapes=[
            pltpu.VMEM((seqs, 256, HEAD), jnp.float32),
            pltpu.VMEM((seqs, 256, HEAD), jnp.float32),
            pltpu.VMEM((seqs, X, HEAD + 8, HEAD), jnp.float32),
            pltpu.VMEM((seqs, HEAD, HEAD), jnp.float32),
            pltpu.VMEM((seqs, HEAD, HEAD), jnp.float32),
            dma((seqs, 3)), dma((seqs, 3)),
            dma((seqs,)), dma((seqs,)),
        ],
        compiler_params=pltpu.CompilerParams(collective_id=1, has_side_effects=True, vmem_limit_bytes=56 * 2**20),
        name="recur",
    )(proj, bias.reshape(1, HEAD), gain.reshape(1, HEAD), sums)


def body(tokens, q_weight, forget_weight, value_weight, forget_bias, norm_gain):
    proj = gather_project(tokens, q_weight, forget_weight, value_weight)
    return recur(proj, forget_bias, norm_gain)


def solution(mesh):
    placed = (
        P(None, "ctx", "zero"),
        P("zero", None),
        P("zero", None),
        P("zero", None),
        P("zero"),
        P("zero"),
    )
    return jax.shard_map(
        body, mesh=mesh, in_specs=placed, out_specs=P(None, "ctx", "zero"), check_vma=False
    )
```

```python
import jax
import jax.numpy as jnp
from jax import lax
from jax.experimental import pallas as pl
from jax.experimental.pallas import tpu as pltpu
from jax.sharding import PartitionSpec as P

MESH = pl.DeviceIdType.MESH
HEAD = 128
TILE = 128
LEVELS = (64, 32, 16, 8, 4, 2, 1)
OFFSETS = (1, 7, 2, 6, 0, 4, 3, 5)
SLOT = {offset: i for i, offset in enumerate(OFFSETS)}
X, Y, Z = 4, 4, 8
HEADS_HERE = 4
UNITS = ((1, 0, 256), (1, 256, 256), (2, 0, 256), (2, 256, 256), (0, 0, 256), (0, 256, 128), (0, 384, 128))
SCHEDULE = (
    ("cross_send",), ("w_send", 0), ("w_send", 1), ("share_affine",), ("sums",), ("ring", 0, 0, 0), ("ring", 1, 0, 0),
    ("a", 0, 0), ("ring", 0, 1, 0), ("b", 0, 0), ("a", 1, 0), ("ring", 1, 1, 0), ("b", 1, 0), ("b", 0, 1), ("a", 0, 1),
    ("w_send", 2), ("a", 1, 1), ("w_send", 3), ("ring", 0, 0, 1), ("b", 1, 1), ("a", 0, 2), ("b", 0, 2), ("a", 1, 2),
    ("b", 1, 2), ("ring", 1, 0, 1), ("ring", 0, 1, 1), ("a", 0, 3), ("b", 0, 3), ("ring", 1, 1, 1), ("a", 2, 0), ("b", 2, 0),
    ("a", 3, 0), ("a", 1, 3), ("b", 1, 3), ("b", 3, 0), ("ready", 0), ("ring", 0, 0, 2), ("a", 2, 1), ("w_send", 4),
    ("b", 2, 1), ("a", 3, 1), ("w_send", 5), ("ring", 1, 0, 2), ("ready", 1), ("b", 3, 1), ("ring", 0, 1, 2), ("a", 2, 2),
    ("b", 2, 2), ("a", 3, 2), ("b", 3, 2), ("ring", 1, 1, 2), ("ring", 0, 0, 3), ("a", 4, 0), ("a", 2, 3), ("b", 2, 3),
    ("b", 4, 0), ("a", 5, 0), ("b", 5, 0), ("ring", 1, 0, 3), ("a", 3, 3), ("b", 3, 3), ("a", 4, 1), ("w_send", 6),
    ("ring", 0, 1, 3), ("ready", 2), ("take_affine",), ("drain", 0), ("drain", 1), ("b", 4, 1), ("ring", 1, 1, 3),
    ("a", 5, 1), ("b", 5, 1), ("ring", 0, 0, 4), ("ring", 1, 0, 4), ("ready", 3), ("a", 6, 0), ("a", 4, 2), ("b", 4, 2),
    ("b", 6, 0), ("a", 5, 2), ("b", 5, 2), ("a", 6, 1), ("ring", 0, 1, 4), ("ring", 1, 1, 4), ("project", 0), ("project", 1),
    ("project", 2), ("a", 4, 3), ("b", 4, 3), ("b", 6, 1), ("project", 3), ("collect", 0), ("collect", 1), ("collect", 2),
    ("b", 5, 3), ("gate", 0), ("a", 6, 2), ("a", 5, 3), ("collect", 3), ("gate", 1), ("gate", 2), ("ready", 4), ("b", 6, 2),
    ("project", 4), ("gate", 3), ("state", 0), ("a", 6, 3), ("collect", 4), ("state", 1), ("ready", 5), ("project", 5),
    ("b", 6, 3), ("state", 2), ("state", 3), ("score", 0), ("ready", 6), ("collect", 5), ("project", 6), ("along_x", 0),
    ("along_x", 1), ("score", 1), ("collect", 6), ("along_x", 2), ("along_x", 3), ("score", 2), ("finish", 0), ("finish", 1),
    ("score", 3), ("finish", 2), ("finish", 3), ("drain", 2), ("drain", 3), ("drain", 4), ("drain", 5), ("drain", 6),
    ("drain_tokens",),
)


def coords():
    c, zi = lax.axis_index("ctx"), lax.axis_index("zero")
    return lax.rem(c, X), c // X, zi // 4, lax.rem(zi // 2, 2), lax.rem(zi, 2)


def place(x, yl, z, yh, k):
    return (yl * X + x, z * 4 + yh * 2 + k)


def wrap(value, n):
    return lax.rem(value + n, n)


def unit_of(weight, head):
    for u, (w, first, count) in enumerate(UNITS):
        if w == weight and first <= head * HEAD < first + count:
            return u, pl.ds(head * HEAD - first, HEAD)


def halves(value):
    high = value.astype(jnp.bfloat16)
    return high, (value - high.astype(jnp.float32)).astype(jnp.bfloat16)


def dot3(a, b, contract):
    (ah, al), (bh, bl) = a, b
    lhs = jnp.concatenate([ah, ah, al], axis=contract[0])
    rhs = jnp.concatenate([bh, bl, bh], axis=contract[1])
    return lax.dot_general(lhs, rhs, (((contract[0],), (contract[1],)), ((), ())), preferred_element_type=jnp.float32)


def log1p_unit(e):
    w = e / (2.0 + e)
    w2 = w * w
    series = jnp.full_like(w2, 1.0 / 17)
    for odd in (15, 13, 11, 9, 7, 5, 3, 1):
        series = series * w2 + 1.0 / odd
    return 2.0 * w * series


def layer_kernel(tok, wq, wf, wv, bias, gain, out, w_all, t_all, acc, other, sums, decays, gates, first_state, local_out, q_decayed,
                 states, total, from_pair, result, affine, own_s, w1_s, w1_r, ag_s, ag_r, y0_s, y0_r, z_s, z_r, p_s, p_r,
                 xs_s, xs_r, ys_s, ys_r, o_s, o_r, f_s, f_r):
    x, yl, z, yh, k = coords()
    z_next, z_prev = wrap(z + 1, Z), wrap(z - 1, Z)
    x_next, x_prev = wrap(x + 1, X), wrap(x - 1, X)
    y = yh * 2 + yl
    y_next, y_prev = wrap(y + 1, Y), wrap(y - 1, Y)
    yh_next, yl_next, yh_prev, yl_prev = y_next // 2, lax.rem(y_next, 2), y_prev // 2, lax.rem(y_prev, 2)
    z_ways = (place(x, yl, z_next, yh, k), place(x, yl, z_prev, yh, k))
    x_ways = (place(x_next, yl, z, yh, k), place(x_prev, yl, z, yh, k))
    y_ways = (place(x, yl_next, z, yh_next, k), place(x, yl_prev, z, yh_prev, k))
    row = (x_ways[0], place(wrap(x + 2, X), yl, z, yh, k), x_ways[1])
    far = place(x, yl, z, 1 - yh, k)
    pair = place(x, 1 - yl, z, yh, k)
    sibling = place(x, yl, z, yh, 1 - k)
    diagonal = place(x, yl, z, 1 - yh, 1 - k)
    mine = yh * 2 + k
    holders = [wrap(z - dz, Z) for dz in OFFSETS]
    owners = [place(x, yl, zt, yh, k) for zt in holders]
    part_a = pl.multiple_of((x * 2 + yl) * 32, 32)
    part_b = pl.multiple_of((yl * X + x) * 32, 32)

    barrier = pltpu.get_barrier_semaphore()
    peers = list(row) + list(y_ways) + [far, sibling, diagonal] + [owners[i] for i in range(Z) if i != SLOT[0]]
    for peer in peers:
        pl.semaphore_signal(barrier, inc=1, device_id=peer, device_id_type=MESH)
    pl.semaphore_wait(barrier, len(peers))

    def remote(src, dst, ss, rs, target):
        return pltpu.make_async_remote_copy(src, dst, ss, rs, device_id=target, device_id_type=MESH)


    def own_tokens(q):
        return pltpu.make_async_copy(tok.at[2 * yh + q], t_all.at[q, SLOT[0], pl.ds(pl.multiple_of(yh * 256, 256), 256)], own_s.at[q])

    def cross(q):
        return remote(tok.at[2 * (1 - yh) + q], t_all.at[q, SLOT[0], pl.ds(pl.multiple_of(yh * 256, 256), 256)],
                      y0_s.at[q], y0_r.at[q], far)

    def hops(q, way):
        return 4 if way == q else 3

    def ring_copy(q, n, way, h):
        sign = (-1, 1)[way]
        here, there = SLOT[sign * (h - 1) % Z], SLOT[sign * h % Z]
        rows = pl.ds(pl.multiple_of((1 - yh if n else yh) * 256, 256), 256)
        return remote(t_all.at[q, here, rows], t_all.at[q, there, rows], z_s.at[q, n, there], z_r.at[q, n, there], z_ways[way])

    def w1(u, i):
        w, first, count = UNITS[u]
        rows = pl.ds(part_a if i < 4 else part_b, 32)
        src = (wq, wf, wv)[w].at[rows, pl.ds(pl.multiple_of(holders[i] * 512 + first, 128), count)]
        dst = w_all.at[w, i, yh, rows, pl.ds(first, count)]
        if i == SLOT[0]:
            return pltpu.make_async_copy(src, dst, own_s.at[2 + u])
        return remote(src, dst, w1_s.at[u, i], w1_r.at[u, i], owners[i])

    def spread(u, step, way):
        w, first, count = UNITS[u]
        forward = step % 2 == 1
        base = 0 if step < 4 else 4
        slots = pl.ds(base + 2 * way, 2) if forward else pl.ds(base, 4)
        yh_from, yl_from = ((yh_prev, yl_prev), (yh_next, yl_next))[way] if forward else (yh, yl)
        x_from = (x_prev, x_next)[way] if forward else x
        if step in (0, 1):
            highs, rows, ways = pl.ds(yh_from, 1), pl.ds(pl.multiple_of((x * 2 + yl_from) * 32, 32), 32), y_ways
        elif step in (2, 3):
            highs, rows, ways = pl.ds(0, 2), pl.ds(pl.multiple_of(x_from * 64, 64), 64), x_ways
        elif step in (4, 5):
            highs, rows, ways = pl.ds(yh, 1), pl.ds(pl.multiple_of((yl * X + x_from) * 32, 32), 32), x_ways
        else:
            highs, rows, ways = pl.ds(yh_from, 1), pl.ds(pl.multiple_of(yl_from * 128, 128), 128), y_ways
        piece = w_all.at[w, slots, highs, rows, pl.ds(first, count)]
        return remote(piece, piece, ag_s.at[u, step, way], ag_r.at[u, step, way], ways[way])

    def partial(u):
        count = UNITS[u][2]
        return remote(acc.at[u, 1 - k, :, pl.ds(0, count)], other.at[u, :, pl.ds(0, count)], p_s.at[u], p_r.at[u], sibling)

    def state_copy(j, way):
        piece = states.at[j, x]
        return remote(piece, piece, xs_s.at[j, way], xs_r.at[j, way], row[way])

    def total_copy(j):
        return remote(total.at[j], from_pair.at[j], ys_s.at[j], ys_r.at[j], pair)

    def result_copy(j):
        return remote(result.at[j], out.at[mine], o_s.at[j], o_r.at[mine], place(x, yl, z, j // 2, j % 2))

    def affine_copy(n):
        piece = affine.at[mine]
        return remote(piece, piece, f_s.at[n], f_r.at[n], (sibling, far, diagonal)[n])


    def both(make, *which):
        for way in range(2):
            make(*which, way).start()

    def wait_both(make, *which):
        for way in range(2):
            make(*which, way).wait_recv()

    def cross_send():
        for q in range(2):
            cross(q).start()

    def w_send(u):
        for i in range(Z):
            w1(u, i).start()

    def ring(q, n, h):
        if h == 0:
            if n == 0:
                own_tokens(q).wait()
            else:
                cross(q).wait_recv()
        for way in range(2):
            if 0 < h <= hops(q, way):
                ring_copy(q, n, way, h).wait_recv()
            if h < hops(q, way):
                ring_copy(q, n, way, h + 1).start()

    def spread_step(half, u, n):
        if n == 0:
            for i in range(4 * half, 4 * half + 4):
                if i == SLOT[0]:
                    w1(u, i).wait()
                else:
                    w1(u, i).wait_recv()
        else:
            wait_both(spread, u, 4 * half + n - 1)
        both(spread, u, 4 * half + n)

    def ready(u):
        wait_both(spread, u, 3)
        wait_both(spread, u, 7)

    def project(u):
        w, first, count = UNITS[u]
        lhs = jnp.concatenate(
            [
                jnp.concatenate([t_all[q, i, pl.ds(high * 256, 256), :] for i in range(Z) for high in range(2)], axis=1)
                for q in range(2)
            ],
            axis=0,
        )
        rhs = w_all[w, :, :, :, pl.ds(first, count)].reshape(Z * 512, count)
        product = jnp.dot(lhs, rhs, preferred_element_type=jnp.float32)
        for q in range(2):
            acc[u, q, :, pl.ds(0, count)] = product[q * 256 : (q + 1) * 256]
        partial(u).start()

    def collect(u):
        partial(u).wait_recv()

    def summed(weight, head):
        u, cols = unit_of(weight, head)
        return acc[u, k, :, cols] + other[u, :, cols]

    t = lax.broadcasted_iota(jnp.int32, (TILE, TILE), 0)
    r = lax.broadcasted_iota(jnp.int32, (TILE, TILE), 1)
    lanes = [slice(u * TILE, (u + 1) * TILE) for u in range(2)]

    def make_sums():
        for i, m in enumerate(LEVELS + (TILE, 0)):
            if m == TILE:
                ones = jnp.where(r <= t, 1.0, 0.0)
            elif m == 0:
                ones = jnp.where(r > t, 1.0, 0.0)
            else:
                start = t // m * m
                after = jnp.where(r >= start, 1.0, 0.0) * jnp.where(r <= t, 1.0, 0.0)
                before = jnp.where(r > t, 1.0, 0.0) * jnp.where(r < start + m, 1.0, 0.0)
                ones = jnp.where((t // m) % 2 == 1, after, before)
            for j in range(3):
                sums[pl.ds(i * TILE, TILE), pl.ds(j * TILE, TILE)] = ones.astype(jnp.bfloat16)

    def gate(j):
        logit = summed(1, j) + affine[j, pl.ds(0, 1), :]
        e = jnp.exp(-jnp.abs(logit))
        log_forget = jnp.minimum(logit, 0.0) - log1p_unit(e)
        gates[j] = jnp.where(logit >= 0.0, e, 1.0) / (1.0 + e)
        wide = jnp.concatenate([log_forget[:TILE], log_forget[TILE:]], axis=1)
        high = wide.astype(jnp.bfloat16)
        rest = wide - high.astype(jnp.float32)
        mid = rest.astype(jnp.bfloat16)
        low = (rest - mid.astype(jnp.float32)).astype(jnp.bfloat16)
        stacked = jnp.concatenate([high, mid, low], axis=0)
        for i in range(len(LEVELS) + 2):
            decays[j, i] = jnp.exp(jnp.dot(sums[pl.ds(i * TILE, TILE), :], stacked, preferred_element_type=jnp.float32))

    def state(j):
        values = summed(2, j)
        own = []
        for u in range(2):
            kept = gates[j, lanes[u], :] * decays[j, len(LEVELS) + 1, :, lanes[u]]
            own.append(dot3(halves(values[lanes[u]]), halves(kept), (0, 0)))
        first_state[j] = own[0]
        own_decay = [decays[j, len(LEVELS), pl.ds(TILE - 1, 1), lanes[u]] for u in range(2)]
        states[j, x, pl.ds(0, HEAD), :] = own[0] * own_decay[1] + own[1]
        states[j, x, pl.ds(HEAD, 8), :] = jnp.broadcast_to(own_decay[0] * own_decay[1], (8, HEAD))
        for way in range(3):
            state_copy(j, way).start()

    def along_x(j):
        for way in range(3):
            state_copy(j, way).wait_recv()
        run = jnp.zeros((HEAD, HEAD), jnp.float32)
        run_decay = jnp.ones((1, HEAD), jnp.float32)
        before, before_decay = run, run_decay
        for xx in range(X):
            before = jnp.where(xx == x, run, before)
            before_decay = jnp.where(xx == x, run_decay, before_decay)
            decay = states[j, xx, pl.ds(HEAD, 1), :]
            run = run * decay + states[j, xx, pl.ds(0, HEAD), :]
            run_decay = run_decay * decay
        total[j] = run
        total_copy(j).start()
        for way in range(3):
            state_copy(j, way).wait_send()
        states[j, x, pl.ds(0, HEAD), :] = before
        states[j, x, pl.ds(HEAD, 8), :] = jnp.broadcast_to(before_decay, (8, HEAD))

    def score(j):
        all_queries, all_values = summed(0, j), summed(2, j)
        queries = [all_queries[rows] for rows in lanes]
        keys = [gates[j, rows, :] for rows in lanes]
        scores = [jnp.where(t == r, jnp.sum(queries[u] * keys[u], axis=1, keepdims=True), 0.0) for u in range(2)]
        for i, m in enumerate(LEVELS):
            upper = (t // m) % 2 == 1
            differ = t ^ r
            mask = (differ >= m) & (differ < 2 * m) & (t > r)
            for u in range(2):
                item = halves(jnp.where(upper, queries[u], keys[u]) * decays[j, i, :, lanes[u]])
                scores[u] = jnp.where(mask, dot3(item, item, (1, 1)), scores[u])
        for u in range(2):
            outputs = dot3(halves(scores[u]), halves(all_values[lanes[u]]), (1, 0))
            decayed = queries[u] * decays[j, len(LEVELS), :, lanes[u]]
            if u == 1:
                outputs = outputs + dot3(halves(decayed), halves(first_state[j]), (1, 1))
                decayed = decayed * decays[j, len(LEVELS), pl.ds(TILE - 1, 1), lanes[0]]
            local_out[j, lanes[u], :] = outputs
            q_decayed[j, lanes[u], :] = decayed

    def finish(j):
        total_copy(j).wait_recv()
        earlier = from_pair[j] * states[j, x, pl.ds(HEAD, 1), :]
        incoming = states[j, x, pl.ds(0, HEAD), :] + jnp.where(yl == 1, earlier, 0.0)
        outputs = local_out[j] + dot3(halves(q_decayed[j]), halves(incoming), (1, 1))
        mean_square = jnp.mean(outputs * outputs, axis=-1, keepdims=True)
        normed = (outputs * lax.rsqrt(mean_square + 1e-05) * affine[j, pl.ds(1, 1), :]).astype(jnp.bfloat16)
        result[j] = normed

        @pl.when(mine == j)
        def _():
            out[mine] = normed

        @pl.when(mine != j)
        def _():
            result_copy(j).start()

    def drain(u):
        for i in range(Z):
            if i != SLOT[0]:
                w1(u, i).wait_send()
        for step in range(8):
            for way in range(2):
                spread(u, step, way).wait_send()

    def drain_tokens():
        for q in range(2):
            cross(q).wait_send()
            for n in range(2):
                for way in range(2):
                    for h in range(1, hops(q, way) + 1):
                        ring_copy(q, n, way, h).wait_send()

    def share_affine():
        affine[mine] = jnp.zeros((8, HEAD), jnp.float32)
        affine[mine, pl.ds(0, 1), :] = bias[...]
        affine[mine, pl.ds(1, 1), :] = gain[...]
        for n in range(3):
            affine_copy(n).start()

    def take_affine():
        for n in range(3):
            affine_copy(n).wait()

    steps = {
        "cross_send": cross_send, "w_send": w_send, "ring": ring, "ready": ready, "project": project, "collect": collect,
        "gate": gate, "state": state, "along_x": along_x, "score": score, "finish": finish, "drain": drain, "drain_tokens": drain_tokens, "share_affine": share_affine, "take_affine": take_affine,
        "a": lambda u, n: spread_step(0, u, n), "b": lambda u, n: spread_step(1, u, n), "sums": make_sums,
    }
    for q in range(2):
        own_tokens(q).start()
    for what, *which in SCHEDULE:
        with jax.named_scope(what):
            steps[what](*which)
    for u in range(len(UNITS)):
        partial(u).wait_send()
    for j in range(HEADS_HERE):
        total_copy(j).wait_send()

        @pl.when(mine != j)
        def _():
            remote(result.at[j], out.at[j], o_s.at[j], o_r.at[j], place(x, yl, z, j // 2, j % 2)).wait()


def body(tokens, q_weight, forget_weight, value_weight, forget_bias, norm_gain):
    seqs = tokens.shape[0]
    dma = pltpu.SemaphoreType.DMA
    any_ = pl.BlockSpec(memory_space=pl.ANY)
    vmem = pl.BlockSpec(memory_space=pltpu.VMEM)
    units = len(UNITS)
    f32, bf16 = jnp.float32, jnp.bfloat16
    return pl.pallas_call(
        layer_kernel,
        out_shape=jax.ShapeDtypeStruct((seqs, 256, HEAD), bf16),
        in_specs=[any_] * 4 + [vmem] * 2,
        out_specs=vmem,
        scratch_shapes=[
            pltpu.VMEM((3, Z, 2, 256, 512), bf16),
            pltpu.VMEM((2, Z, 512, 256), bf16),
            pltpu.VMEM((units, 2, 256, 256), f32),
            pltpu.VMEM((units, 256, 256), f32),
            pltpu.VMEM(((len(LEVELS) + 2) * TILE, 3 * TILE), bf16),
            pltpu.VMEM((HEADS_HERE, len(LEVELS) + 2, TILE, 2 * TILE), f32),
            pltpu.VMEM((HEADS_HERE, 256, HEAD), f32),
            pltpu.VMEM((HEADS_HERE, HEAD, HEAD), f32),
            pltpu.VMEM((HEADS_HERE, 256, HEAD), f32),
            pltpu.VMEM((HEADS_HERE, 256, HEAD), f32),
            pltpu.VMEM((HEADS_HERE, X, HEAD + 8, HEAD), f32),
            pltpu.VMEM((HEADS_HERE, HEAD, HEAD), f32),
            pltpu.VMEM((HEADS_HERE, HEAD, HEAD), f32),
            pltpu.VMEM((HEADS_HERE, 256, HEAD), bf16),
            pltpu.VMEM((HEADS_HERE, 8, HEAD), f32),
            dma((2 + units,)),
            dma((units, Z)), dma((units, Z)),
            dma((units, 8, 2)), dma((units, 8, 2)),
            dma((2,)), dma((2,)),
            dma((2, 2, Z)), dma((2, 2, Z)),
            dma((units,)), dma((units,)),
            dma((HEADS_HERE, 3)), dma((HEADS_HERE, 3)),
            dma((HEADS_HERE,)), dma((HEADS_HERE,)),
            dma((HEADS_HERE,)), dma((HEADS_HERE,)),
            dma((3,)), dma((3,)),
        ],
        compiler_params=pltpu.CompilerParams(collective_id=0, has_side_effects=True, vmem_limit_bytes=56 * 2**20),
        name="layer",
    )(tokens, q_weight, forget_weight, value_weight, forget_bias.reshape(1, HEAD), norm_gain.reshape(1, HEAD))


def solution(mesh):
    placed = (
        P(None, "ctx", "zero"),
        P("zero", None),
        P("zero", None),
        P("zero", None),
        P("zero"),
        P("zero"),
    )
    return jax.shard_map(
        body, mesh=mesh, in_specs=placed, out_specs=P(None, "ctx", "zero"), check_vma=False
    )
```

```python
import jax
import jax.numpy as jnp
from jax import lax
from jax.experimental import pallas as pl
from jax.experimental.pallas import tpu as pltpu
from jax.sharding import PartitionSpec as P

MESH = pl.DeviceIdType.MESH
HEAD = 128
TILE = 128
LEVELS = (64, 32, 16, 8, 4, 2, 1)
OFFSETS = (1, 7, 2, 6, 0, 4, 3, 5)
SLOT = {offset: i for i, offset in enumerate(OFFSETS)}
X, Y, Z = 4, 4, 8
HEADS_HERE = 4
UNITS = ((1, 0, 256), (1, 256, 256), (2, 0, 256), (2, 256, 256), (0, 0, 256), (0, 256, 256))
PRODUCTS = ((1, 0, 512), (2, 0, 512), (0, 0, 512))
SCHEDULE = (
    ("cross_send",), ("w_send", 0), ("w_send", 1), ("share_affine",), ("sums",), ("a", 0, 0), ("w_send", 2),
    ("ring", 0, 0, 0), ("ring", 1, 0, 0), ("ring", 0, 1, 0), ("b", 0, 0), ("a", 1, 0), ("w_send", 3), ("ring", 1, 1, 0),
    ("b", 1, 0), ("a", 0, 1), ("a", 2, 0), ("b", 0, 1), ("a", 1, 1), ("b", 2, 0), ("b", 1, 1), ("a", 0, 2), ("b", 0, 2),
    ("a", 2, 1), ("ring", 0, 0, 1), ("a", 1, 2), ("w_send", 4), ("b", 2, 1), ("b", 1, 2), ("ring", 1, 0, 1),
    ("ring", 0, 1, 1), ("a", 3, 0), ("b", 0, 3), ("a", 0, 3), ("a", 2, 2), ("w_send", 5), ("b", 3, 0), ("ring", 1, 1, 1),
    ("a", 1, 3), ("b", 1, 3), ("b", 2, 2), ("ring", 0, 0, 2), ("a", 3, 1), ("a", 4, 0), ("b", 4, 0), ("ready", 0),
    ("ring", 1, 0, 2), ("a", 2, 3), ("ring", 0, 1, 2), ("a", 5, 0), ("b", 3, 1), ("b", 5, 0), ("b", 2, 3), ("ready", 1),
    ("a", 3, 2), ("b", 4, 1), ("ring", 1, 1, 2), ("a", 4, 1), ("project", 0, 0, 5), ("a", 5, 1), ("ring", 0, 0, 3),
    ("b", 3, 2), ("ready", 2), ("take_affine",), ("b", 5, 1), ("a", 4, 2), ("ring", 1, 0, 3), ("ring", 0, 1, 3), ("a", 3, 3),
    ("a", 5, 2), ("b", 4, 2), ("ring", 1, 1, 3), ("b", 3, 3), ("b", 5, 2), ("ring", 0, 0, 4), ("ring", 1, 0, 4),
    ("ring", 0, 1, 4), ("ring", 1, 1, 4), ("project", 0, 5, 8), ("a", 4, 3), ("b", 4, 3), ("collect", 0), ("gate", 2),
    ("gate", 3), ("gate", 1), ("ready", 3), ("project", 1, 0, 5), ("project", 1, 5, 8), ("gate", 0), ("a", 5, 3),
    ("collect", 1), ("state", 2), ("b", 5, 3), ("state", 3), ("state", 1), ("state", 0), ("ready", 4), ("along_pair", 2),
    ("ready", 5), ("along_pair", 3), ("project", 2, 0, 8), ("along_pair", 1), ("along_pair", 0), ("along_x", 2),
    ("along_x", 3), ("collect", 2), ("score", 2), ("along_x", 1), ("score", 3), ("along_x", 0), ("finish", 2), ("score", 1),
    ("finish", 3), ("score", 0), ("finish", 1), ("finish", 0), ("drain",),
)


def coords():
    c, zi = lax.axis_index("ctx"), lax.axis_index("zero")
    return lax.rem(c, X), c // X, zi // 4, lax.rem(zi // 2, 2), lax.rem(zi, 2)


def place(x, yl, z, yh, k):
    return (yl * X + x, z * 4 + yh * 2 + k)


def wrap(value, n):
    return lax.rem(value + n, n)


def halves(value):
    high = value.astype(jnp.bfloat16)
    return high, (value - high.astype(jnp.float32)).astype(jnp.bfloat16)


def dot3(a, b, contract):
    (ah, al), (bh, bl) = a, b
    lhs = jnp.concatenate([ah, ah, al], axis=contract[0])
    rhs = jnp.concatenate([bh, bl, bh], axis=contract[1])
    return lax.dot_general(lhs, rhs, (((contract[0],), (contract[1],)), ((), ())), preferred_element_type=jnp.float32)


def log1p_unit(e):
    w = e / (2.0 + e)
    w2 = w * w
    series = jnp.full_like(w2, 1.0 / 17)
    for odd in (15, 13, 11, 9, 7, 5, 3, 1):
        series = series * w2 + 1.0 / odd
    return 2.0 * w * series


def layer_kernel(tok, wq, wf, wv, bias, gain, out, w_all, t_all, acc, other, sums, decays, gates, first_state, local_out, q_decayed,
                 states, total, from_pair, result, affine, own_s, w1_s, w1_r, ag_s, ag_r, y0_r, t_s, z_r, p_s, p_r,
                 xs_s, xs_r, ys_s, ys_r, o_s, o_r, f_s, f_r):
    x, yl, z, yh, k = coords()
    z_next, z_prev = wrap(z + 1, Z), wrap(z - 1, Z)
    x_next, x_prev = wrap(x + 1, X), wrap(x - 1, X)
    y = yh * 2 + yl
    y_next, y_prev = wrap(y + 1, Y), wrap(y - 1, Y)
    yh_next, yl_next, yh_prev, yl_prev = y_next // 2, lax.rem(y_next, 2), y_prev // 2, lax.rem(y_prev, 2)
    z_ways = (place(x, yl, z_next, yh, k), place(x, yl, z_prev, yh, k))
    x_ways = (place(x_next, yl, z, yh, k), place(x_prev, yl, z, yh, k))
    y_ways = (place(x, yl_next, z, yh_next, k), place(x, yl_prev, z, yh_prev, k))
    odd = lax.rem(x, 2)
    row = (place(x + 1 - 2 * odd, yl, z, yh, k), place(X - 1 - x, yl, z, yh, k))
    far = place(x, yl, z, 1 - yh, k)
    pair = place(x, 1 - yl, z, yh, k)
    sibling = place(x, yl, z, yh, 1 - k)
    diagonal = place(x, yl, z, 1 - yh, 1 - k)
    mine = yh * 2 + k
    heads = (mine, yh * 2 + 1 - k, (1 - yh) * 2 + k, (1 - yh) * 2 + 1 - k)
    owner_of = (None, sibling, far, diagonal)
    holders = [wrap(z - dz, Z) for dz in OFFSETS]
    owners = [place(x, yl, zt, yh, k) for zt in holders]
    part_a = pl.multiple_of((x * 2 + yl) * 32, 32)
    part_b = pl.multiple_of((yl * X + x) * 32, 32)

    barrier = pltpu.get_barrier_semaphore()
    peers = list(x_ways) + list(y_ways) + [far, sibling, diagonal] + [owners[i] for i in range(Z) if i != SLOT[0]]
    for peer in peers:
        pl.semaphore_signal(barrier, inc=1, device_id=peer, device_id_type=MESH)
    pl.semaphore_wait(barrier, len(peers))

    def remote(src, dst, ss, rs, target):
        return pltpu.make_async_remote_copy(src, dst, ss, rs, device_id=target, device_id_type=MESH)


    def own_tokens():
        return pltpu.make_async_copy(tok.at[pl.ds(2 * yh, 2)], t_all.at[:, SLOT[0], pl.ds(pl.multiple_of(yh * 256, 256), 256)], own_s)

    def cross(q):
        return remote(tok.at[2 * (1 - yh) + q], t_all.at[q, SLOT[0], pl.ds(pl.multiple_of(yh * 256, 256), 256)],
                      t_s, y0_r.at[q], far)

    def hops(q, way):
        return 4 if way == q else 3

    def ring_copy(q, n, way, h):
        sign = (-1, 1)[way]
        here, there = SLOT[sign * (h - 1) % Z], SLOT[sign * h % Z]
        rows = pl.ds(pl.multiple_of((1 - yh if n else yh) * 256, 256), 256)
        return remote(t_all.at[q, here, rows], t_all.at[q, there, rows], t_s, z_r.at[q, n, h - 1], z_ways[way])

    def w1(u, i):
        w, first, count = UNITS[u]
        rows = pl.ds(part_a if i < 4 else part_b, 32)
        src = (wq, wf, wv)[w].at[rows, pl.ds(pl.multiple_of(holders[i] * 512 + first, 128), count)]
        dst = w_all.at[w, i, yh, rows, pl.ds(first, count)]
        if i == SLOT[0]:
            return pltpu.make_async_copy(src, dst, w1_r.at[u, i // 4])
        return remote(src, dst, w1_s, w1_r.at[u, i // 4], owners[i])

    def spread(u, step, way):
        w, first, count = UNITS[u]
        forward = step % 2 == 1
        base = 0 if step < 4 else 4
        slots = pl.ds(base + 2 * way, 2) if forward else pl.ds(base, 4)
        yh_from, yl_from = ((yh_prev, yl_prev), (yh_next, yl_next))[way] if forward else (yh, yl)
        x_from = (x_prev, x_next)[way] if forward else x
        if step in (0, 1):
            highs, rows, ways = pl.ds(yh_from, 1), pl.ds(pl.multiple_of((x * 2 + yl_from) * 32, 32), 32), y_ways
        elif step in (2, 3):
            highs, rows, ways = pl.ds(0, 2), pl.ds(pl.multiple_of(x_from * 64, 64), 64), x_ways
        elif step in (4, 5):
            highs, rows, ways = pl.ds(yh, 1), pl.ds(pl.multiple_of((yl * X + x_from) * 32, 32), 32), x_ways
        else:
            highs, rows, ways = pl.ds(yh_from, 1), pl.ds(pl.multiple_of(yl_from * 128, 128), 128), y_ways
        piece = w_all.at[w, slots, highs, rows, pl.ds(first, count)]
        return remote(piece, piece, ag_s, ag_r.at[u, step], ways[way])

    def partial(p):
        w, first, count = PRODUCTS[p]
        cols = pl.ds(w * 512 + first, count)
        return remote(acc.at[1 - k, :, cols], other.at[:, cols], p_s, p_r.at[p], sibling)

    def state_copy(j, step):
        return remote(states.at[j, 2 * step], states.at[j, 2 * step + 1], xs_s, xs_r.at[j, step], row[step])

    def total_copy(j):
        return remote(total.at[j], from_pair.at[j], ys_s, ys_r.at[j], pair)

    def result_copy(j):
        return remote(result.at[j], out.at[mine], o_s, o_r, owner_of[j])

    def affine_copy(n):
        piece = affine.at[mine]
        return remote(piece, piece, f_s, f_r, owner_of[1 + n])

    def arrived(piece, sem):
        remote(piece, piece, t_s, sem, far).wait_recv()

    def left_here(piece, sem):
        remote(piece, piece, sem, y0_r.at[0], far).wait_send()


    def both(make, *which):
        for way in range(2):
            make(*which, way).start()

    def wait_both(u, step):
        w, first, count = UNITS[u]
        slots, highs, rows = ((8, 1, 32), (4, 1, 32), (8, 2, 64), (4, 2, 64), (8, 1, 32), (4, 1, 32), (8, 1, 128), (4, 1, 128))[step]
        arrived(w_all.at[w, pl.ds(0, slots), pl.ds(0, highs), pl.ds(0, rows), pl.ds(first, count)], ag_r.at[u, step])

    def cross_send():
        for q in range(2):
            cross(q).start()

    def w_send(u):
        for i in range(Z):
            w1(u, i).start()

    def ring(q, n, h):
        if h == 0:
            if n:
                cross(q).wait_recv()
            elif q == 0:
                own_tokens().wait()
        else:
            ways = sum(h <= hops(q, way) for way in range(2))
            arrived(t_all.at[0, 0, pl.ds(0, 256 * ways)], z_r.at[q, n, h - 1])
        for way in range(2):
            if h < hops(q, way):
                ring_copy(q, n, way, h + 1).start()

    def spread_step(half, u, n):
        if n == 0:
            w, first, count = UNITS[u]
            arrived(w_all.at[w, pl.ds(0, 4), 0, pl.ds(0, 32), pl.ds(first, count)], w1_r.at[u, half])
        else:
            wait_both(u, 4 * half + n - 1)
        both(spread, u, 4 * half + n)

    def ready(u):
        wait_both(u, 3)
        wait_both(u, 7)

    def project(p, begin, end):
        w, first, count = PRODUCTS[p]
        lhs = jnp.concatenate(
            [
                jnp.concatenate([t_all[q, i, pl.ds(high * 256, 256), :] for i in range(begin, end) for high in range(2)], axis=1)
                for q in range(2)
            ],
            axis=0,
        )
        rhs = w_all[w, pl.ds(begin, end - begin), :, :, pl.ds(first, count)].reshape((end - begin) * 512, count)
        product = jnp.dot(lhs, rhs, preferred_element_type=jnp.float32)
        cols = pl.ds(w * 512 + first, count)
        for q in range(2):
            rows = product[q * 256 : (q + 1) * 256]
            acc[q, :, cols] = acc[q, :, cols] + rows if begin else rows
        if end == Z:
            partial(p).start()

    def collect(p):
        partial(p).wait_recv()

    def summed(weight, head):
        cols = pl.ds(pl.multiple_of(weight * 512 + heads[head] * HEAD, HEAD), HEAD)
        return acc[k, :, cols] + other[:, cols]

    t = lax.broadcasted_iota(jnp.int32, (TILE, TILE), 0)
    r = lax.broadcasted_iota(jnp.int32, (TILE, TILE), 1)
    lanes = [slice(u * TILE, (u + 1) * TILE) for u in range(2)]

    def make_sums():
        for i, m in enumerate(LEVELS + (TILE, 0)):
            if m == TILE:
                ones = jnp.where(r <= t, 1.0, 0.0)
            elif m == 0:
                ones = jnp.where(r > t, 1.0, 0.0)
            else:
                start = t // m * m
                after = jnp.where(r >= start, 1.0, 0.0) * jnp.where(r <= t, 1.0, 0.0)
                before = jnp.where(r > t, 1.0, 0.0) * jnp.where(r < start + m, 1.0, 0.0)
                ones = jnp.where((t // m) % 2 == 1, after, before)
            for j in range(3):
                sums[pl.ds(i * TILE, TILE), pl.ds(j * TILE, TILE)] = ones.astype(jnp.bfloat16)

    def gate(j):
        logit = summed(1, j) + affine[heads[j], pl.ds(0, 1), :]
        e = jnp.exp(-jnp.abs(logit))
        log_forget = jnp.minimum(logit, 0.0) - log1p_unit(e)
        gates[j] = jnp.where(logit >= 0.0, e, 1.0) / (1.0 + e)
        wide = jnp.concatenate([log_forget[:TILE], log_forget[TILE:]], axis=1)
        high = wide.astype(jnp.bfloat16)
        rest = wide - high.astype(jnp.float32)
        mid = rest.astype(jnp.bfloat16)
        low = (rest - mid.astype(jnp.float32)).astype(jnp.bfloat16)
        stacked = jnp.concatenate([high, mid, low], axis=0)
        for i in range(len(LEVELS) + 2):
            decays[j, i] = jnp.exp(jnp.dot(sums[pl.ds(i * TILE, TILE), :], stacked, preferred_element_type=jnp.float32))

    def state(j):
        values = summed(2, j)
        own = []
        for u in range(2):
            kept = gates[j, lanes[u], :] * decays[j, len(LEVELS) + 1, :, lanes[u]]
            own.append(dot3(halves(values[lanes[u]]), halves(kept), (0, 0)))
        first_state[j] = own[0]
        own_decay = [decays[j, len(LEVELS), pl.ds(TILE - 1, 1), lanes[u]] for u in range(2)]
        put_state(j, 0, own[0] * own_decay[1] + own[1], own_decay[0] * own_decay[1])
        state_copy(j, 0).start()

    def put_state(j, n, value, decay):
        states[j, n, pl.ds(0, HEAD), :] = value
        states[j, n, pl.ds(HEAD, 8), :] = jnp.broadcast_to(decay, (8, HEAD))

    def get_state(j, n):
        return states[j, n, pl.ds(0, HEAD), :], states[j, n, pl.ds(HEAD, 1), :]

    def along_pair(j):
        state_copy(j, 0).wait_recv()
        (own, own_decay), (mate, mate_decay) = get_state(j, 0), get_state(j, 1)
        after = odd == 1
        joined = jnp.where(after, mate * own_decay + own, own * mate_decay + mate)
        put_state(j, 2, joined, own_decay * mate_decay)
        state_copy(j, 1).start()

    def along_x(j):
        state_copy(j, 1).wait_recv()
        (mate, mate_decay), (own, own_decay), (pairs, pairs_decay) = get_state(j, 1), get_state(j, 2), get_state(j, 3)
        second, after = x >= 2, odd == 1
        total[j] = jnp.where(second, pairs * own_decay + own, own * pairs_decay + pairs)
        total_copy(j).start()
        near, near_decay = jnp.where(after, mate, 0.0), jnp.where(after, mate_decay, 1.0)
        put_state(j, 4, near + jnp.where(second, pairs * near_decay, 0.0), jnp.where(second, pairs_decay * near_decay, near_decay))

    def score(j):
        all_queries, all_values = summed(0, j), summed(2, j)
        queries = [all_queries[rows] for rows in lanes]
        keys = [gates[j, rows, :] for rows in lanes]
        scores = [jnp.where(t == r, jnp.sum(queries[u] * keys[u], axis=1, keepdims=True), 0.0) for u in range(2)]
        for i, m in enumerate(LEVELS):
            upper = (t // m) % 2 == 1
            differ = t ^ r
            mask = (differ >= m) & (differ < 2 * m) & (t > r)
            for u in range(2):
                item = halves(jnp.where(upper, queries[u], keys[u]) * decays[j, i, :, lanes[u]])
                scores[u] = jnp.where(mask, dot3(item, item, (1, 1)), scores[u])
        for u in range(2):
            outputs = dot3(halves(scores[u]), halves(all_values[lanes[u]]), (1, 0))
            decayed = queries[u] * decays[j, len(LEVELS), :, lanes[u]]
            if u == 1:
                outputs = outputs + dot3(halves(decayed), halves(first_state[j]), (1, 1))
                decayed = decayed * decays[j, len(LEVELS), pl.ds(TILE - 1, 1), lanes[0]]
            local_out[j, lanes[u], :] = outputs
            q_decayed[j, lanes[u], :] = decayed

    def finish(j):
        total_copy(j).wait_recv()
        row_state, row_decay = get_state(j, 4)
        incoming = row_state + jnp.where(yl == 1, from_pair[j] * row_decay, 0.0)
        outputs = local_out[j] + dot3(halves(q_decayed[j]), halves(incoming), (1, 1))
        mean_square = jnp.mean(outputs * outputs, axis=-1, keepdims=True)
        normed = (outputs * lax.rsqrt(mean_square + 1e-05) * affine[heads[j], pl.ds(1, 1), :]).astype(jnp.bfloat16)
        if j == 0:
            out[mine] = normed
        else:
            result[j] = normed
            result_copy(j).start()

    def drain():
        left_here(w_all.at[:, pl.ds(0, Z - 1), 0, pl.ds(0, 32)], w1_s)
        left_here(w_all.at[:, :, :, pl.ds(0, 240)], ag_s)
        left_here(t_all.at[:, :, pl.ds(0, 480)], t_s)
        left_here(acc.at[0, :, pl.ds(0, 3 * 512)], p_s)
        left_here(states.at[:, pl.ds(0, 2)], xs_s)
        left_here(total, ys_s)
        left_here(result.at[pl.ds(0, 3)], o_s)
        left_here(affine.at[pl.ds(0, 3)], f_s)

    def share_affine():
        affine[mine] = jnp.zeros((8, HEAD), jnp.float32)
        affine[mine, pl.ds(0, 1), :] = bias[...]
        affine[mine, pl.ds(1, 1), :] = gain[...]
        for n in range(3):
            affine_copy(n).start()

    def take_affine():
        arrived(affine.at[pl.ds(0, 3)], f_r)

    steps = {
        "cross_send": cross_send, "w_send": w_send, "ring": ring, "ready": ready, "project": project, "collect": collect,
        "gate": gate, "state": state, "along_pair": along_pair, "along_x": along_x, "score": score, "finish": finish, "drain": drain, "share_affine": share_affine, "take_affine": take_affine,
        "a": lambda u, n: spread_step(0, u, n), "b": lambda u, n: spread_step(1, u, n), "sums": make_sums,
    }
    own_tokens().start()
    for what, *which in SCHEDULE:
        with jax.named_scope(what):
            steps[what](*which)
    arrived(result.at[pl.ds(0, 3)], o_r)


def body(tokens, q_weight, forget_weight, value_weight, forget_bias, norm_gain):
    seqs = tokens.shape[0]
    dma = pltpu.SemaphoreType.DMA
    any_ = pl.BlockSpec(memory_space=pl.ANY)
    vmem = pl.BlockSpec(memory_space=pltpu.VMEM)
    units = len(UNITS)
    f32, bf16 = jnp.float32, jnp.bfloat16
    return pl.pallas_call(
        layer_kernel,
        out_shape=jax.ShapeDtypeStruct((seqs, 256, HEAD), bf16),
        in_specs=[any_] * 4 + [vmem] * 2,
        out_specs=vmem,
        scratch_shapes=[
            pltpu.VMEM((3, Z, 2, 256, 512), bf16),
            pltpu.VMEM((2, Z, 512, 256), bf16),
            pltpu.VMEM((2, 256, 3 * 512), f32),
            pltpu.VMEM((256, 3 * 512), f32),
            pltpu.VMEM(((len(LEVELS) + 2) * TILE, 3 * TILE), bf16),
            pltpu.VMEM((HEADS_HERE, len(LEVELS) + 2, TILE, 2 * TILE), f32),
            pltpu.VMEM((HEADS_HERE, 256, HEAD), f32),
            pltpu.VMEM((HEADS_HERE, HEAD, HEAD), f32),
            pltpu.VMEM((HEADS_HERE, 256, HEAD), f32),
            pltpu.VMEM((HEADS_HERE, 256, HEAD), f32),
            pltpu.VMEM((HEADS_HERE, 5, HEAD + 8, HEAD), f32),
            pltpu.VMEM((HEADS_HERE, HEAD, HEAD), f32),
            pltpu.VMEM((HEADS_HERE, HEAD, HEAD), f32),
            pltpu.VMEM((HEADS_HERE, 256, HEAD), bf16),
            pltpu.VMEM((HEADS_HERE, 8, HEAD), f32),
            dma,
            dma, dma((units, 2)),
            dma, dma((units, 8)),
            dma((2,)), dma, dma((2, 2, 4)),
            dma, dma((len(PRODUCTS),)),
            dma, dma((HEADS_HERE, 2)),
            dma, dma((HEADS_HERE,)),
            dma, dma,
            dma, dma,
        ],
        compiler_params=pltpu.CompilerParams(collective_id=0, has_side_effects=True, vmem_limit_bytes=56 * 2**20),
        name="layer",
    )(tokens, q_weight, forget_weight, value_weight, forget_bias.reshape(1, HEAD), norm_gain.reshape(1, HEAD))


def solution(mesh):
    placed = (
        P(None, "ctx", "zero"),
        P("zero", None),
        P("zero", None),
        P("zero", None),
        P("zero"),
        P("zero"),
    )
    return jax.shard_map(
        body, mesh=mesh, in_specs=placed, out_specs=P(None, "ctx", "zero"), check_vma=False
    )
```

```python
import jax
import jax.numpy as jnp
from jax import lax
from jax.experimental import pallas as pl
from jax.experimental.pallas import tpu as pltpu
from jax.sharding import PartitionSpec as P

MESH = pl.DeviceIdType.MESH
HEAD = 128
TILE = 128
LEVELS = (64, 32, 16, 8, 4, 2, 1)
OFFSETS = (4, 3, 5, 1, 7, 2, 6, 0)
SLOT = {offset: i for i, offset in enumerate(OFFSETS)}
X, Y, Z = 4, 4, 8
HEADS_HERE = 4
UNITS = ((1, 0, 256), (1, 256, 256), (2, 0, 256), (2, 256, 256), (0, 0, 256), (0, 256, 256))
Y_FIRST = (4, 3, 4, 3, 4, 3)
PRODUCTS = ((1, 0, 512), (2, 0, 512), (0, 0, 512))
SCHEDULE = (
    ("cross_send",), ("w_send", 0, 1), ("own_send", 0), ("w_send", 1, 0), ("own_send", 1), ("w_send", 0, 0),
    ("share_affine",), ("sums",), ("b", 0, 0), ("w_send", 3, 0), ("a", 1, 0), ("w_send", 2, 1), ("w_send", 3, 1),
    ("own_send", 3), ("a", 0, 0), ("b", 0, 1), ("w_send", 1, 1), ("w_send", 2, 0), ("a", 3, 0), ("own_step", 0),
    ("own_step", 1), ("b", 2, 0), ("w_send", 5, 1), ("b", 0, 2), ("a", 1, 1), ("own_send", 2), ("b", 3, 0), ("own_step", 3),
    ("b", 1, 0), ("ring", 0, 0, 0), ("ring", 0, 1, 0), ("ring", 1, 0, 0), ("ring", 1, 1, 0), ("a", 0, 1), ("b", 2, 1),
    ("a", 2, 0), ("a", 3, 1), ("b", 5, 0), ("b", 3, 1), ("w_send", 4, 0), ("b", 1, 1), ("ring", 0, 0, 1), ("b", 5, 1),
    ("b", 0, 3), ("b", 2, 2), ("w_send", 5, 0), ("b", 1, 2), ("ring", 0, 1, 1), ("a", 1, 2), ("own_step", 2), ("a", 0, 2),
    ("ring", 1, 0, 1), ("a", 2, 1), ("ring", 1, 1, 1), ("a", 1, 3), ("w_send", 4, 1), ("a", 3, 2), ("a", 4, 0), ("b", 2, 3),
    ("ring", 0, 0, 2), ("a", 5, 0), ("a", 0, 3), ("ring", 0, 1, 2), ("b", 1, 3), ("b", 3, 2), ("a", 2, 2), ("ring", 1, 0, 2),
    ("a", 4, 1), ("a", 3, 3), ("own_send", 4), ("ring", 1, 1, 2), ("a", 5, 1), ("b", 4, 0), ("ready", 0), ("ready", 1),
    ("project", 0, 3, 8), ("ring", 0, 0, 3), ("ring", 0, 1, 3), ("a", 2, 3), ("own_send", 5), ("b", 3, 3), ("b", 5, 2),
    ("ring", 1, 0, 3), ("b", 4, 1), ("a", 4, 2), ("own_step", 4), ("a", 5, 2), ("own_step", 5), ("ring", 1, 1, 3),
    ("ready", 2), ("take_affine",), ("b", 4, 2), ("ready", 3), ("project", 1, 3, 8), ("ring", 0, 0, 4), ("ring", 1, 0, 4),
    ("ring", 0, 1, 4), ("ring", 1, 1, 4), ("project", 0, 0, 3), ("project", 1, 0, 3), ("collect", 0), ("gate", 2),
    ("gate", 3), ("a", 4, 3), ("collect", 1), ("state", 2), ("state", 3), ("gate", 1), ("state", 1), ("b", 5, 3), ("gate", 0),
    ("state", 0), ("levels", 2), ("levels", 3), ("a", 5, 3), ("levels", 1), ("levels", 0), ("b", 4, 3), ("along_pair", 2),
    ("along_pair", 3), ("along_pair", 1), ("ready", 4), ("along_x", 2), ("along_pair", 0), ("ready", 5), ("along_x", 3),
    ("project_in_turn", 2), ("along_x", 1), ("collect", 2), ("score", 2), ("along_x", 0), ("finish", 2), ("score", 3),
    ("finish", 3), ("score", 1), ("finish", 1), ("score", 0), ("finish", 0), ("drain",),
)


def coords():
    c, zi = lax.axis_index("ctx"), lax.axis_index("zero")
    return lax.rem(c, X), c // X, zi // 4, lax.rem(zi // 2, 2), lax.rem(zi, 2)


def place(x, yl, z, yh, k):
    return (yl * X + x, z * 4 + yh * 2 + k)


def wrap(value, n):
    return lax.rem(value + n, n)


def halves(value):
    high = value.astype(jnp.bfloat16)
    return high, (value - high.astype(jnp.float32)).astype(jnp.bfloat16)


def dot3(a, b, contract):
    (ah, al), (bh, bl) = a, b
    lhs = jnp.concatenate([ah, ah, al], axis=contract[0])
    rhs = jnp.concatenate([bh, bl, bh], axis=contract[1])
    return lax.dot_general(lhs, rhs, (((contract[0],), (contract[1],)), ((), ())), preferred_element_type=jnp.float32)


def log1p_unit(e):
    w = e / (2.0 + e)
    w2 = w * w
    series = jnp.full_like(w2, 1.0 / 17)
    for odd in (15, 13, 11, 9, 7, 5, 3, 1):
        series = series * w2 + 1.0 / odd
    return 2.0 * w * series


def layer_kernel(tok, wq, wf, wv, bias, gain, out, w_all, t_all, acc, other, sums, logs, decays, gates, first_state, local_out, q_decayed,
                 states, total, from_pair, result, affine, own_s, wo_r, e_s, e_r, w1_s, w1_r, ag_s, ag_r, y0_r, t_s, z_r, p_s, p_r,
                 xs_s, xs_r, ys_s, ys_r, o_s, o_r, f_s, f_r):
    x, yl, z, yh, k = coords()
    z_next, z_prev = wrap(z + 1, Z), wrap(z - 1, Z)
    x_next, x_prev = wrap(x + 1, X), wrap(x - 1, X)
    y = yh * 2 + yl
    y_next, y_prev = wrap(y + 1, Y), wrap(y - 1, Y)
    yh_next, yl_next, yh_prev, yl_prev = y_next // 2, lax.rem(y_next, 2), y_prev // 2, lax.rem(y_prev, 2)
    z_ways = (place(x, yl, z_next, yh, k), place(x, yl, z_prev, yh, k))
    x_ways = (place(x_next, yl, z, yh, k), place(x_prev, yl, z, yh, k))
    y_ways = (place(x, yl_next, z, yh_next, k), place(x, yl_prev, z, yh_prev, k))
    odd = lax.rem(x, 2)
    row = (place(x + 1 - 2 * odd, yl, z, yh, k), place(X - 1 - x, yl, z, yh, k))
    far = place(x, yl, z, 1 - yh, k)
    pair = place(x, 1 - yl, z, yh, k)
    opposite = place(x, 1 - yl, z, 1 - yh, k)
    sibling = place(x, yl, z, yh, 1 - k)
    diagonal = place(x, yl, z, 1 - yh, 1 - k)
    mine = yh * 2 + k
    heads = (mine, yh * 2 + 1 - k, (1 - yh) * 2 + k, (1 - yh) * 2 + 1 - k)
    owner_of = (None, sibling, far, diagonal)
    holders = [wrap(z - dz, Z) for dz in OFFSETS]
    owners = [place(x, yl, zt, yh, k) for zt in holders]
    part_a = pl.multiple_of((x * 2 + yl) * 32, 32)
    part_b = pl.multiple_of((yl * X + x) * 32, 32)

    barrier = pltpu.get_barrier_semaphore()
    peers = list(x_ways) + list(y_ways) + [far, sibling, diagonal] + [owners[i] for i in range(Z) if i != SLOT[0]]
    for peer in peers:
        pl.semaphore_signal(barrier, inc=1, device_id=peer, device_id_type=MESH)
    pl.semaphore_wait(barrier, len(peers))

    def remote(src, dst, ss, rs, target):
        return pltpu.make_async_remote_copy(src, dst, ss, rs, device_id=target, device_id_type=MESH)


    def own_tokens():
        return pltpu.make_async_copy(tok.at[pl.ds(2 * yh, 2)], t_all.at[:, SLOT[0], pl.ds(pl.multiple_of(yh * 256, 256), 256)], own_s)

    def cross(q):
        return remote(tok.at[2 * (1 - yh) + q], t_all.at[q, SLOT[0], pl.ds(pl.multiple_of(yh * 256, 256), 256)],
                      t_s, y0_r.at[q], far)

    def hops(q, way):
        return 4 if way == q else 3

    def ring_copy(q, n, way, h):
        sign = (-1, 1)[way]
        here, there = SLOT[sign * (h - 1) % Z], SLOT[sign * h % Z]
        rows = pl.ds(pl.multiple_of((1 - yh if n else yh) * 256, 256), 256)
        return remote(t_all.at[q, here, rows], t_all.at[q, there, rows], t_s, z_r.at[q, n, h - 1], z_ways[way])

    def source(u, z_to, rows):
        w, first, count = UNITS[u]
        return (wq, wf, wv)[w].at[rows, pl.ds(pl.multiple_of(z_to * 512 + first, 128), count)]

    def w1(u, i):
        w, first, count = UNITS[u]
        half = int(i >= Y_FIRST[u])
        rows = pl.ds((part_a, part_b)[half], 32)
        return remote(source(u, holders[i], rows), w_all.at[w, i, yh, rows, pl.ds(first, count)], w1_s, w1_r.at[u, half], owners[i])

    def own_rows(u):
        w, first, count = UNITS[u]
        return pltpu.make_async_copy(source(u, z, pl.ds(0, 256)), w_all.at[w, SLOT[0], yh, :, pl.ds(first, count)], wo_r.at[u])

    def other_rows(u, step):
        w, first, count = UNITS[u]
        half = pl.ds(pl.multiple_of((yl if step else 1 - yl) * 128, 128), 128)
        dst = w_all.at[w, SLOT[0], 1 - yh if step else yh, half, pl.ds(first, count)]
        return remote(dst if step else source(u, z, half), dst, e_s, e_r.at[u, step], pair if step else opposite)

    def spread(u, step, way):
        w, first, count = UNITS[u]
        forward = step % 2 == 1
        slots = pl.ds(0, Y_FIRST[u]) if step < 4 else pl.ds(Y_FIRST[u], Z - 1 - Y_FIRST[u])
        cols = pl.ds(first + way * (count // 2), count // 2) if forward else pl.ds(first, count)
        yh_from, yl_from = ((yh_prev, yl_prev), (yh_next, yl_next))[way] if forward else (yh, yl)
        x_from = (x_prev, x_next)[way] if forward else x
        if step in (0, 1):
            highs, rows, ways = pl.ds(yh_from, 1), pl.ds(pl.multiple_of((x * 2 + yl_from) * 32, 32), 32), y_ways
        elif step in (2, 3):
            highs, rows, ways = pl.ds(0, 2), pl.ds(pl.multiple_of(x_from * 64, 64), 64), x_ways
        elif step in (4, 5):
            highs, rows, ways = pl.ds(yh, 1), pl.ds(pl.multiple_of((yl * X + x_from) * 32, 32), 32), x_ways
        else:
            highs, rows, ways = pl.ds(yh_from, 1), pl.ds(pl.multiple_of(yl_from * 128, 128), 128), y_ways
        piece = w_all.at[w, slots, highs, rows, cols]
        return remote(piece, piece, ag_s, ag_r.at[u, step], ways[way])

    def partial(p):
        w, first, count = PRODUCTS[p]
        cols = pl.ds(w * 512 + first, count)
        return remote(acc.at[1 - k, :, cols], other.at[:, cols], p_s, p_r.at[p], sibling)

    def state_copy(j, step):
        return remote(states.at[j, 2 * step], states.at[j, 2 * step + 1], xs_s, xs_r.at[j, step], row[step])

    def total_copy(j):
        return remote(total.at[j], from_pair.at[j], ys_s, ys_r.at[j], pair)

    def result_copy(j):
        return remote(result.at[j], out.at[mine], o_s, o_r, owner_of[j])

    def affine_copy(n):
        piece = affine.at[mine]
        return remote(piece, piece, f_s, f_r, owner_of[1 + n])

    def arrived(piece, sem):
        remote(piece, piece, t_s, sem, far).wait_recv()

    def left_here(piece, sem):
        remote(piece, piece, sem, y0_r.at[0], far).wait_send()


    def both(make, *which):
        for way in range(2):
            make(*which, way).start()

    def wait_both(u, step):
        w, first, count = UNITS[u]
        slots = Y_FIRST[u] if step < 4 else Z - 1 - Y_FIRST[u]
        rows = (32, 32, 128, 128, 32, 32, 128, 128)[step] * (1 if step % 2 else 2)
        arrived(w_all.at[w, pl.ds(0, slots), 0, pl.ds(0, rows), pl.ds(first, count)], ag_r.at[u, step])

    def cross_send():
        for q in range(2):
            cross(q).start()

    def w_send(u, half):
        for i in range(Y_FIRST[u], Z - 1) if half else range(Y_FIRST[u]):
            w1(u, i).start()

    def own_send(u):
        other_rows(u, 0).start()
        own_rows(u).start()

    def own_step(u):
        other_rows(u, 0).wait_recv()
        other_rows(u, 1).start()

    def ring(q, n, h):
        if h == 0:
            if n:
                cross(q).wait_recv()
            elif q == 0:
                own_tokens().wait()
        else:
            ways = sum(h <= hops(q, way) for way in range(2))
            arrived(t_all.at[0, 0, pl.ds(0, 256 * ways)], z_r.at[q, n, h - 1])
        for way in range(2):
            if h < hops(q, way):
                ring_copy(q, n, way, h + 1).start()

    def spread_step(half, u, n):
        if n == 0:
            w, first, count = UNITS[u]
            slots = Z - 1 - Y_FIRST[u] if half else Y_FIRST[u]
            arrived(w_all.at[w, pl.ds(0, slots), 0, pl.ds(0, 32), pl.ds(first, count)], w1_r.at[u, half])
        else:
            wait_both(u, 4 * half + n - 1)
        both(spread, u, 4 * half + n)

    def ready(u):
        wait_both(u, 3)
        wait_both(u, 7)
        own_rows(u).wait()
        other_rows(u, 1).wait_recv()

    def project(p, begin, end):
        w, first, count = PRODUCTS[p]
        lhs = jnp.concatenate(
            [
                jnp.concatenate([t_all[q, i, pl.ds(high * 256, 256), :] for i in range(begin, end) for high in range(2)], axis=1)
                for q in range(2)
            ],
            axis=0,
        )
        rhs = w_all[w, pl.ds(begin, end - begin), :, :, pl.ds(first, count)].reshape((end - begin) * 512, count)
        product = jnp.dot(lhs, rhs, preferred_element_type=jnp.float32)
        cols = pl.ds(w * 512 + first, count)
        for q in range(2):
            rows = product[q * 256 : (q + 1) * 256]
            acc[q, :, cols] = rows if end == Z else acc[q, :, cols] + rows
        if begin == 0:
            partial(p).start()

    def project_in_turn(p):
        w, first, count = PRODUCTS[p]
        cols = pl.ds(w * 512 + first, count)
        rhs = w_all[w, :, :, :, pl.ds(first, count)].reshape(Z * 512, count)
        for q in (1 - k, k):
            lhs = jnp.concatenate([t_all[q, i, pl.ds(high * 256, 256), :] for i in range(Z) for high in range(2)], axis=1)
            acc[q, :, cols] = jnp.dot(lhs, rhs, preferred_element_type=jnp.float32)
            if q is not k:
                partial(p).start()

    def collect(p):
        partial(p).wait_recv()

    def summed(weight, head):
        cols = pl.ds(pl.multiple_of(weight * 512 + heads[head] * HEAD, HEAD), HEAD)
        return acc[k, :, cols] + other[:, cols]

    t = lax.broadcasted_iota(jnp.int32, (TILE, TILE), 0)
    r = lax.broadcasted_iota(jnp.int32, (TILE, TILE), 1)
    lanes = [slice(u * TILE, (u + 1) * TILE) for u in range(2)]

    def make_sums():
        for i, m in enumerate(LEVELS + (TILE, 0)):
            if m == TILE:
                ones = jnp.where(r <= t, 1.0, 0.0)
            elif m == 0:
                ones = jnp.where(r > t, 1.0, 0.0)
            else:
                start = t // m * m
                after = jnp.where(r >= start, 1.0, 0.0) * jnp.where(r <= t, 1.0, 0.0)
                before = jnp.where(r > t, 1.0, 0.0) * jnp.where(r < start + m, 1.0, 0.0)
                ones = jnp.where((t // m) % 2 == 1, after, before)
            for j in range(3):
                sums[pl.ds(i * TILE, TILE), pl.ds(j * TILE, TILE)] = ones.astype(jnp.bfloat16)

    def gate(j):
        logit = summed(1, j) + affine[heads[j], pl.ds(0, 1), :]
        e = jnp.exp(-jnp.abs(logit))
        log_forget = jnp.minimum(logit, 0.0) - log1p_unit(e)
        gates[j] = jnp.where(logit >= 0.0, e, 1.0) / (1.0 + e)
        wide = jnp.concatenate([log_forget[:TILE], log_forget[TILE:]], axis=1)
        high = wide.astype(jnp.bfloat16)
        rest = wide - high.astype(jnp.float32)
        mid = rest.astype(jnp.bfloat16)
        low = (rest - mid.astype(jnp.float32)).astype(jnp.bfloat16)
        logs[j] = jnp.concatenate([high, mid, low], axis=0)
        fill_decays(j, len(LEVELS), len(LEVELS) + 2)

    def fill_decays(j, begin, end):
        for i in range(begin, end):
            decays[j, i] = jnp.exp(jnp.dot(sums[pl.ds(i * TILE, TILE), :], logs[j], preferred_element_type=jnp.float32))

    def levels(j):
        fill_decays(j, 0, len(LEVELS))

    def state(j):
        values = summed(2, j)
        own = []
        for u in range(2):
            kept = gates[j, lanes[u], :] * decays[j, len(LEVELS) + 1, :, lanes[u]]
            own.append(dot3(halves(values[lanes[u]]), halves(kept), (0, 0)))
        first_state[j] = own[0]
        own_decay = [decays[j, len(LEVELS), pl.ds(TILE - 1, 1), lanes[u]] for u in range(2)]
        put_state(j, 0, own[0] * own_decay[1] + own[1], own_decay[0] * own_decay[1])
        state_copy(j, 0).start()

    def put_state(j, n, value, decay):
        states[j, n, pl.ds(0, HEAD), :] = value
        states[j, n, pl.ds(HEAD, 8), :] = jnp.broadcast_to(decay, (8, HEAD))

    def get_state(j, n):
        return states[j, n, pl.ds(0, HEAD), :], states[j, n, pl.ds(HEAD, 1), :]

    def along_pair(j):
        state_copy(j, 0).wait_recv()
        (own, own_decay), (mate, mate_decay) = get_state(j, 0), get_state(j, 1)
        after = odd == 1
        joined = jnp.where(after, mate * own_decay + own, own * mate_decay + mate)
        put_state(j, 2, joined, own_decay * mate_decay)
        state_copy(j, 1).start()

    def along_x(j):
        state_copy(j, 1).wait_recv()
        (mate, mate_decay), (own, own_decay), (pairs, pairs_decay) = get_state(j, 1), get_state(j, 2), get_state(j, 3)
        second, after = x >= 2, odd == 1
        total[j] = jnp.where(second, pairs * own_decay + own, own * pairs_decay + pairs)
        total_copy(j).start()
        near, near_decay = jnp.where(after, mate, 0.0), jnp.where(after, mate_decay, 1.0)
        put_state(j, 4, near + jnp.where(second, pairs * near_decay, 0.0), jnp.where(second, pairs_decay * near_decay, near_decay))

    def score(j):
        all_queries, all_values = summed(0, j), summed(2, j)
        queries = [all_queries[rows] for rows in lanes]
        keys = [gates[j, rows, :] for rows in lanes]
        scores = [jnp.where(t == r, jnp.sum(queries[u] * keys[u], axis=1, keepdims=True), 0.0) for u in range(2)]
        for i, m in enumerate(LEVELS):
            upper = (t // m) % 2 == 1
            differ = t ^ r
            mask = (differ >= m) & (differ < 2 * m) & (t > r)
            for u in range(2):
                item = halves(jnp.where(upper, queries[u], keys[u]) * decays[j, i, :, lanes[u]])
                scores[u] = jnp.where(mask, dot3(item, item, (1, 1)), scores[u])
        for u in range(2):
            outputs = dot3(halves(scores[u]), halves(all_values[lanes[u]]), (1, 0))
            decayed = queries[u] * decays[j, len(LEVELS), :, lanes[u]]
            if u == 1:
                outputs = outputs + dot3(halves(decayed), halves(first_state[j]), (1, 1))
                decayed = decayed * decays[j, len(LEVELS), pl.ds(TILE - 1, 1), lanes[0]]
            local_out[j, lanes[u], :] = outputs
            q_decayed[j, lanes[u], :] = decayed

    def finish(j):
        total_copy(j).wait_recv()
        row_state, row_decay = get_state(j, 4)
        incoming = row_state + jnp.where(yl == 1, from_pair[j] * row_decay, 0.0)
        outputs = local_out[j] + dot3(halves(q_decayed[j]), halves(incoming), (1, 1))
        mean_square = jnp.mean(outputs * outputs, axis=-1, keepdims=True)
        normed = (outputs * lax.rsqrt(mean_square + 1e-05) * affine[heads[j], pl.ds(1, 1), :]).astype(jnp.bfloat16)
        if j == 0:
            out[mine] = normed
        else:
            result[j] = normed
            result_copy(j).start()

    def drain():
        left_here(w_all.at[:, pl.ds(0, Z - 1), 0, pl.ds(0, 32)], w1_s)
        left_here(w_all.at[:, pl.ds(0, Z - 1), :, pl.ds(0, 240)], ag_s)
        left_here(w_all.at[:, 0, 0], e_s)
        left_here(t_all.at[:, :, pl.ds(0, 480)], t_s)
        left_here(acc.at[0, :, pl.ds(0, 3 * 512)], p_s)
        left_here(states.at[:, pl.ds(0, 2)], xs_s)
        left_here(total, ys_s)
        left_here(result.at[pl.ds(0, 3)], o_s)
        left_here(affine.at[pl.ds(0, 3)], f_s)

    def share_affine():
        affine[mine] = jnp.zeros((8, HEAD), jnp.float32)
        affine[mine, pl.ds(0, 1), :] = bias[...]
        affine[mine, pl.ds(1, 1), :] = gain[...]
        for n in range(3):
            affine_copy(n).start()

    def take_affine():
        arrived(affine.at[pl.ds(0, 3)], f_r)

    steps = {
        "cross_send": cross_send, "w_send": w_send, "own_send": own_send, "own_step": own_step, "ring": ring, "ready": ready, "project": project, "project_in_turn": project_in_turn, "collect": collect,
        "gate": gate, "levels": levels, "state": state, "along_pair": along_pair, "along_x": along_x, "score": score, "finish": finish, "drain": drain, "share_affine": share_affine, "take_affine": take_affine,
        "a": lambda u, n: spread_step(0, u, n), "b": lambda u, n: spread_step(1, u, n), "sums": make_sums,
    }
    own_tokens().start()
    for what, *which in SCHEDULE:
        with jax.named_scope(what):
            steps[what](*which)
    arrived(result.at[pl.ds(0, 3)], o_r)


def body(tokens, q_weight, forget_weight, value_weight, forget_bias, norm_gain):
    seqs = tokens.shape[0]
    dma = pltpu.SemaphoreType.DMA
    any_ = pl.BlockSpec(memory_space=pl.ANY)
    vmem = pl.BlockSpec(memory_space=pltpu.VMEM)
    units = len(UNITS)
    f32, bf16 = jnp.float32, jnp.bfloat16
    return pl.pallas_call(
        layer_kernel,
        out_shape=pltpu.VMEM((seqs, 256, HEAD), bf16),
        in_specs=[any_] * 4 + [vmem] * 2,
        out_specs=vmem,
        scratch_shapes=[
            pltpu.VMEM((3, Z, 2, 256, 512), bf16),
            pltpu.VMEM((2, Z, 512, 256), bf16),
            pltpu.VMEM((2, 256, 3 * 512), f32),
            pltpu.VMEM((256, 3 * 512), f32),
            pltpu.VMEM(((len(LEVELS) + 2) * TILE, 3 * TILE), bf16),
            pltpu.VMEM((HEADS_HERE, 3 * TILE, 2 * TILE), bf16),
            pltpu.VMEM((HEADS_HERE, len(LEVELS) + 2, TILE, 2 * TILE), f32),
            pltpu.VMEM((HEADS_HERE, 256, HEAD), f32),
            pltpu.VMEM((HEADS_HERE, HEAD, HEAD), f32),
            pltpu.VMEM((HEADS_HERE, 256, HEAD), f32),
            pltpu.VMEM((HEADS_HERE, 256, HEAD), f32),
            pltpu.VMEM((HEADS_HERE, 5, HEAD + 8, HEAD), f32),
            pltpu.VMEM((HEADS_HERE, HEAD, HEAD), f32),
            pltpu.VMEM((HEADS_HERE, HEAD, HEAD), f32),
            pltpu.VMEM((HEADS_HERE, 256, HEAD), bf16),
            pltpu.VMEM((HEADS_HERE, 8, HEAD), f32),
            dma, dma((units,)),
            dma, dma((units, 2)),
            dma, dma((units, 2)),
            dma, dma((units, 8)),
            dma((2,)), dma, dma((2, 2, 4)),
            dma, dma((len(PRODUCTS),)),
            dma, dma((HEADS_HERE, 2)),
            dma, dma((HEADS_HERE,)),
            dma, dma,
            dma, dma,
        ],
        compiler_params=pltpu.CompilerParams(collective_id=0, has_side_effects=True, vmem_limit_bytes=56 * 2**20),
        name="layer",
    )(tokens, q_weight, forget_weight, value_weight, forget_bias.reshape(1, HEAD), norm_gain.reshape(1, HEAD))


def solution(mesh):
    placed = (
        P(None, "ctx", "zero"),
        P("zero", None),
        P("zero", None),
        P("zero", None),
        P("zero"),
        P("zero"),
    )
    return jax.shard_map(
        body, mesh=mesh, in_specs=placed, out_specs=P(None, "ctx", "zero"), check_vma=False
    )
```

```python
import jax
import jax.numpy as jnp
from jax import lax
from jax.experimental import pallas as pl
from jax.experimental.pallas import tpu as pltpu
from jax.sharding import PartitionSpec as P

MESH = pl.DeviceIdType.MESH
HEAD = 128
TILE = 128
LEVELS = (64, 32, 16, 8, 4, 2, 1)
OFFSETS = (4, 3, 5, 1, 7, 2, 6, 0)
SLOT = {offset: i for i, offset in enumerate(OFFSETS)}
X, Y, Z = 4, 4, 8
HEADS_HERE = 4
UNITS = ((1, 0, 128), (1, 128, 128), (1, 256, 256), (2, 0, 256), (2, 256, 256), (0, 0, 256), (0, 256, 256))
Y_FIRST = (4, 4, 4, 3, 4, 3, 3)
PRODUCTS = ((1, 0, 512), (2, 0, 512), (0, 0, 512))
SCHEDULE = (
    ("cross_send",), ("w_send", 0, 1), ("share_affine",), ("sums",), ("w_send", 6, 1), ("w_send", 0, 0), ("own_send", 0),
    ("w_send", 1, 0), ("w_send", 3, 0), ("own_send", 5), ("b", 0, 0), ("w_send", 3, 1), ("w_send", 4, 1), ("w_send", 2, 0),
    ("b", 6, 0), ("a", 0, 0), ("a", 1, 0), ("b", 0, 1), ("w_send", 1, 1), ("a", 3, 0), ("b", 6, 1), ("own_step", 0),
    ("b", 3, 0), ("b", 0, 2), ("w_send", 2, 1), ("w_send", 4, 0), ("own_step", 5), ("b", 4, 0), ("a", 0, 1), ("a", 1, 1),
    ("a", 2, 0), ("a", 3, 1), ("w_send", 6, 0), ("b", 1, 0), ("ring", 0, 0, 0), ("ring", 0, 1, 0), ("ring", 1, 0, 0),
    ("ring", 1, 1, 0), ("b", 3, 1), ("b", 2, 0), ("w_send", 5, 0), ("b", 4, 1), ("b", 0, 3), ("a", 4, 0), ("b", 1, 1),
    ("a", 0, 2), ("own_send", 1), ("a", 1, 2), ("own_send", 2), ("a", 6, 0), ("b", 2, 1), ("a", 2, 1), ("b", 1, 2),
    ("ring", 0, 0, 1), ("a", 4, 1), ("own_step", 1), ("a", 0, 3), ("own_step", 2), ("ring", 0, 1, 1), ("a", 6, 1),
    ("a", 2, 2), ("a", 1, 3), ("a", 3, 2), ("b", 2, 2), ("own_send", 4), ("ring", 1, 0, 1), ("b", 1, 3), ("ready", 0),
    ("b", 3, 2), ("ring", 1, 1, 1), ("a", 5, 0), ("a", 2, 3), ("a", 4, 2), ("w_send", 5, 1), ("own_send", 6), ("b", 2, 3),
    ("own_send", 3), ("b", 4, 2), ("ring", 0, 0, 2), ("own_step", 4), ("ready", 1), ("ring", 0, 1, 2), ("a", 3, 3),
    ("ring", 1, 0, 2), ("b", 3, 3), ("a", 5, 1), ("ring", 1, 1, 2), ("b", 5, 0), ("own_step", 6), ("own_step", 3),
    ("ready", 2), ("take_affine",), ("project", 0, 3, 8), ("a", 4, 3), ("a", 6, 2), ("ring", 0, 0, 3), ("ring", 0, 1, 3),
    ("b", 4, 3), ("b", 6, 2), ("b", 5, 1), ("ring", 1, 0, 3), ("a", 5, 2), ("ready", 3), ("ring", 1, 1, 3), ("ready", 4),
    ("project", 1, 3, 8), ("a", 6, 3), ("b", 5, 2), ("ring", 0, 0, 4), ("ring", 1, 0, 4), ("ring", 0, 1, 4),
    ("ring", 1, 1, 4), ("project", 0, 0, 3), ("project", 1, 0, 3), ("b", 6, 3), ("a", 5, 3), ("collect", 0), ("gate", 2),
    ("gate", 3), ("gate", 1), ("collect", 1), ("state", 2), ("state", 3), ("state", 1), ("gate", 0), ("state", 0),
    ("levels", 2), ("levels", 3), ("levels", 1), ("levels", 0), ("b", 5, 3), ("along_pair", 2), ("along_pair", 3),
    ("ready", 6), ("along_pair", 1), ("along_x", 2), ("along_pair", 0), ("ready", 5), ("along_x", 3), ("project_in_turn", 2),
    ("along_x", 1), ("along_x", 0), ("collect", 2), ("score", 2), ("finish", 2), ("score", 3), ("finish", 3), ("score", 1),
    ("finish", 1), ("score", 0), ("finish", 0), ("drain",),
)


def coords():
    c, zi = lax.axis_index("ctx"), lax.axis_index("zero")
    return lax.rem(c, X), c // X, zi // 4, lax.rem(zi // 2, 2), lax.rem(zi, 2)


def place(x, yl, z, yh, k):
    return (yl * X + x, z * 4 + yh * 2 + k)


def wrap(value, n):
    return lax.rem(value + n, n)


def halves(value):
    high = value.astype(jnp.bfloat16)
    return high, (value - high.astype(jnp.float32)).astype(jnp.bfloat16)


def dot3(a, b, contract):
    (ah, al), (bh, bl) = a, b
    lhs = jnp.concatenate([ah, ah, al], axis=contract[0])
    rhs = jnp.concatenate([bh, bl, bh], axis=contract[1])
    return lax.dot_general(lhs, rhs, (((contract[0],), (contract[1],)), ((), ())), preferred_element_type=jnp.float32)


def log1p_unit(e):
    w = e / (2.0 + e)
    w2 = w * w
    series = jnp.full_like(w2, 1.0 / 17)
    for odd in (15, 13, 11, 9, 7, 5, 3, 1):
        series = series * w2 + 1.0 / odd
    return 2.0 * w * series


def layer_kernel(tok, wq, wf, wv, bias, gain, out, w_all, t_all, acc, other, sums, logs, decays, gates, first_state, local_out, q_decayed,
                 states, total, from_pair, result, affine, own_s, wo_r, e_s, e_r, w1_s, w1_r, ag_s, ag_r, y0_r, t_s, z_r, p_s, p_r,
                 xs_s, xs_r, ys_s, ys_r, o_s, o_r, f_s, f_r):
    x, yl, z, yh, k = coords()
    z_next, z_prev = wrap(z + 1, Z), wrap(z - 1, Z)
    x_next, x_prev = wrap(x + 1, X), wrap(x - 1, X)
    y = yh * 2 + yl
    y_next, y_prev = wrap(y + 1, Y), wrap(y - 1, Y)
    yh_next, yl_next, yh_prev, yl_prev = y_next // 2, lax.rem(y_next, 2), y_prev // 2, lax.rem(y_prev, 2)
    z_ways = (place(x, yl, z_next, yh, k), place(x, yl, z_prev, yh, k))
    x_ways = (place(x_next, yl, z, yh, k), place(x_prev, yl, z, yh, k))
    y_ways = (place(x, yl_next, z, yh_next, k), place(x, yl_prev, z, yh_prev, k))
    odd = lax.rem(x, 2)
    row = (place(x + 1 - 2 * odd, yl, z, yh, k), place(X - 1 - x, yl, z, yh, k))
    far = place(x, yl, z, 1 - yh, k)
    pair = place(x, 1 - yl, z, yh, k)
    opposite = place(x, 1 - yl, z, 1 - yh, k)
    sibling = place(x, yl, z, yh, 1 - k)
    diagonal = place(x, yl, z, 1 - yh, 1 - k)
    mine = yh * 2 + k
    heads = (mine, yh * 2 + 1 - k, (1 - yh) * 2 + k, (1 - yh) * 2 + 1 - k)
    owner_of = (None, sibling, far, diagonal)
    holders = [wrap(z - dz, Z) for dz in OFFSETS]
    owners = [place(x, yl, zt, yh, k) for zt in holders]
    part_a = pl.multiple_of((x * 2 + yl) * 32, 32)
    part_b = pl.multiple_of((yl * X + x) * 32, 32)

    barrier = pltpu.get_barrier_semaphore()
    peers = list(x_ways) + list(y_ways) + [far, sibling, diagonal] + [owners[i] for i in range(Z) if i != SLOT[0]]
    for peer in peers:
        pl.semaphore_signal(barrier, inc=1, device_id=peer, device_id_type=MESH)
    pl.semaphore_wait(barrier, len(peers))

    def remote(src, dst, ss, rs, target):
        return pltpu.make_async_remote_copy(src, dst, ss, rs, device_id=target, device_id_type=MESH)


    def own_tokens():
        return pltpu.make_async_copy(tok.at[pl.ds(2 * yh, 2)], t_all.at[:, SLOT[0], pl.ds(pl.multiple_of(yh * 256, 256), 256)], own_s)

    def cross(q):
        return remote(tok.at[2 * (1 - yh) + q], t_all.at[q, SLOT[0], pl.ds(pl.multiple_of(yh * 256, 256), 256)],
                      t_s, y0_r.at[q], far)

    def hops(q, way):
        return 4 if way == q else 3

    def ring_copy(q, n, way, h):
        sign = (-1, 1)[way]
        here, there = SLOT[sign * (h - 1) % Z], SLOT[sign * h % Z]
        rows = pl.ds(pl.multiple_of((1 - yh if n else yh) * 256, 256), 256)
        return remote(t_all.at[q, here, rows], t_all.at[q, there, rows], t_s, z_r.at[q, n, h - 1], z_ways[way])

    def source(u, z_to, rows):
        w, first, count = UNITS[u]
        return (wq, wf, wv)[w].at[rows, pl.ds(pl.multiple_of(z_to * 512 + first, 128), count)]

    def w1(u, i):
        w, first, count = UNITS[u]
        half = int(i >= Y_FIRST[u])
        rows = pl.ds((part_a, part_b)[half], 32)
        return remote(source(u, holders[i], rows), w_all.at[w, i, yh, rows, pl.ds(first, count)], w1_s, w1_r.at[u, half], owners[i])

    def own_rows(u):
        w, first, count = UNITS[u]
        return pltpu.make_async_copy(source(u, z, pl.ds(0, 256)), w_all.at[w, SLOT[0], yh, :, pl.ds(first, count)], wo_r.at[u])

    def other_rows(u, step):
        w, first, count = UNITS[u]
        half = pl.ds(pl.multiple_of((yl if step else 1 - yl) * 128, 128), 128)
        dst = w_all.at[w, SLOT[0], 1 - yh if step else yh, half, pl.ds(first, count)]
        return remote(dst if step else source(u, z, half), dst, e_s, e_r.at[u, step], pair if step else opposite)

    def spread(u, step, way):
        w, first, count = UNITS[u]
        forward = step % 2 == 1
        begin, end = (0, Y_FIRST[u]) if step < 4 else (Y_FIRST[u], Z - 1)
        if forward and count > 128:
            first, count = first + way * (count // 2), count // 2
        elif forward:
            middle = (begin + end + 1) // 2
            begin, end = (middle, end) if way else (begin, middle)
        slots, cols = pl.ds(begin, end - begin), pl.ds(first, count)
        yh_from, yl_from = ((yh_prev, yl_prev), (yh_next, yl_next))[way] if forward else (yh, yl)
        x_from = (x_prev, x_next)[way] if forward else x
        if step in (0, 1):
            highs, rows, ways = pl.ds(yh_from, 1), pl.ds(pl.multiple_of((x * 2 + yl_from) * 32, 32), 32), y_ways
        elif step in (2, 3):
            highs, rows, ways = pl.ds(0, 2), pl.ds(pl.multiple_of(x_from * 64, 64), 64), x_ways
        elif step in (4, 5):
            highs, rows, ways = pl.ds(yh, 1), pl.ds(pl.multiple_of((yl * X + x_from) * 32, 32), 32), x_ways
        else:
            highs, rows, ways = pl.ds(yh_from, 1), pl.ds(pl.multiple_of(yl_from * 128, 128), 128), y_ways
        piece = w_all.at[w, slots, highs, rows, cols]
        return remote(piece, piece, ag_s, ag_r.at[u, step], ways[way])

    def partial(p):
        w, first, count = PRODUCTS[p]
        cols = pl.ds(w * 512 + first, count)
        return remote(acc.at[1 - k, :, cols], other.at[:, cols], p_s, p_r.at[p], sibling)

    def state_copy(j, step):
        return remote(states.at[j, 2 * step], states.at[j, 2 * step + 1], xs_s, xs_r.at[j, step], row[step])

    def total_copy(j):
        return remote(total.at[j], from_pair.at[j], ys_s, ys_r.at[j], pair)

    def result_copy(j):
        return remote(result.at[j], out.at[mine], o_s, o_r, owner_of[j])

    def affine_copy(n):
        piece = affine.at[mine]
        return remote(piece, piece, f_s, f_r, owner_of[1 + n])

    def arrived(piece, sem):
        remote(piece, piece, t_s, sem, far).wait_recv()

    def left_here(piece, sem):
        remote(piece, piece, sem, y0_r.at[0], far).wait_send()


    def both(make, *which):
        for way in range(2):
            make(*which, way).start()

    def wait_both(u, step):
        w, first, count = UNITS[u]
        slots = Y_FIRST[u] if step < 4 else Z - 1 - Y_FIRST[u]
        rows = (32, 32, 128, 128, 32, 32, 128, 128)[step] * (1 if step % 2 else 2)
        arrived(w_all.at[w, pl.ds(0, slots), 0, pl.ds(0, rows), pl.ds(first, count)], ag_r.at[u, step])

    def cross_send():
        for q in range(2):
            cross(q).start()

    def w_send(u, half):
        for i in range(Y_FIRST[u], Z - 1) if half else range(Y_FIRST[u]):
            w1(u, i).start()

    def own_send(u):
        other_rows(u, 0).start()
        own_rows(u).start()

    def own_step(u):
        other_rows(u, 0).wait_recv()
        other_rows(u, 1).start()

    def ring(q, n, h):
        if h == 0:
            if n:
                cross(q).wait_recv()
            elif q == 0:
                own_tokens().wait()
        else:
            ways = sum(h <= hops(q, way) for way in range(2))
            arrived(t_all.at[0, 0, pl.ds(0, 256 * ways)], z_r.at[q, n, h - 1])
        for way in range(2):
            if h < hops(q, way):
                ring_copy(q, n, way, h + 1).start()

    def spread_step(half, u, n):
        if n == 0:
            w, first, count = UNITS[u]
            slots = Z - 1 - Y_FIRST[u] if half else Y_FIRST[u]
            arrived(w_all.at[w, pl.ds(0, slots), 0, pl.ds(0, 32), pl.ds(first, count)], w1_r.at[u, half])
        else:
            wait_both(u, 4 * half + n - 1)
        both(spread, u, 4 * half + n)

    def ready(u):
        wait_both(u, 3)
        wait_both(u, 7)
        own_rows(u).wait()
        other_rows(u, 1).wait_recv()

    def project(p, begin, end):
        w, first, count = PRODUCTS[p]
        lhs = jnp.concatenate(
            [
                jnp.concatenate([t_all[q, i, pl.ds(high * 256, 256), :] for i in range(begin, end) for high in range(2)], axis=1)
                for q in range(2)
            ],
            axis=0,
        )
        rhs = w_all[w, pl.ds(begin, end - begin), :, :, pl.ds(first, count)].reshape((end - begin) * 512, count)
        product = jnp.dot(lhs, rhs, preferred_element_type=jnp.float32)
        cols = pl.ds(w * 512 + first, count)
        for q in range(2):
            rows = product[q * 256 : (q + 1) * 256]
            acc[q, :, cols] = rows if end == Z else acc[q, :, cols] + rows
        if begin == 0:
            partial(p).start()

    def project_in_turn(p):
        w, first, count = PRODUCTS[p]
        cols = pl.ds(w * 512 + first, count)
        rhs = w_all[w, :, :, :, pl.ds(first, count)].reshape(Z * 512, count)
        for q in (1 - k, k):
            lhs = jnp.concatenate([t_all[q, i, pl.ds(high * 256, 256), :] for i in range(Z) for high in range(2)], axis=1)
            acc[q, :, cols] = jnp.dot(lhs, rhs, preferred_element_type=jnp.float32)
            if q is not k:
                partial(p).start()

    def collect(p):
        partial(p).wait_recv()

    def summed(weight, head):
        cols = pl.ds(pl.multiple_of(weight * 512 + heads[head] * HEAD, HEAD), HEAD)
        return acc[k, :, cols] + other[:, cols]

    t = lax.broadcasted_iota(jnp.int32, (TILE, TILE), 0)
    r = lax.broadcasted_iota(jnp.int32, (TILE, TILE), 1)
    lanes = [slice(u * TILE, (u + 1) * TILE) for u in range(2)]

    def make_sums():
        for i, m in enumerate(LEVELS + (TILE, 0)):
            if m == TILE:
                ones = jnp.where(r <= t, 1.0, 0.0)
            elif m == 0:
                ones = jnp.where(r > t, 1.0, 0.0)
            else:
                start = t // m * m
                after = jnp.where(r >= start, 1.0, 0.0) * jnp.where(r <= t, 1.0, 0.0)
                before = jnp.where(r > t, 1.0, 0.0) * jnp.where(r < start + m, 1.0, 0.0)
                ones = jnp.where((t // m) % 2 == 1, after, before)
            for j in range(3):
                sums[pl.ds(i * TILE, TILE), pl.ds(j * TILE, TILE)] = ones.astype(jnp.bfloat16)

    def gate(j):
        logit = summed(1, j) + affine[heads[j], pl.ds(0, 1), :]
        e = jnp.exp(-jnp.abs(logit))
        log_forget = jnp.minimum(logit, 0.0) - log1p_unit(e)
        gates[j] = jnp.where(logit >= 0.0, e, 1.0) / (1.0 + e)
        wide = jnp.concatenate([log_forget[:TILE], log_forget[TILE:]], axis=1)
        high = wide.astype(jnp.bfloat16)
        rest = wide - high.astype(jnp.float32)
        mid = rest.astype(jnp.bfloat16)
        low = (rest - mid.astype(jnp.float32)).astype(jnp.bfloat16)
        logs[j] = jnp.concatenate([high, mid, low], axis=0)
        fill_decays(j, len(LEVELS), len(LEVELS) + 2)

    def fill_decays(j, begin, end):
        for i in range(begin, end):
            decays[j, i] = jnp.exp(jnp.dot(sums[pl.ds(i * TILE, TILE), :], logs[j], preferred_element_type=jnp.float32))

    def levels(j):
        fill_decays(j, 0, len(LEVELS))

    def state(j):
        values = summed(2, j)
        own = []
        for u in range(2):
            kept = gates[j, lanes[u], :] * decays[j, len(LEVELS) + 1, :, lanes[u]]
            own.append(dot3(halves(values[lanes[u]]), halves(kept), (0, 0)))
        first_state[j] = own[0]
        own_decay = [decays[j, len(LEVELS), pl.ds(TILE - 1, 1), lanes[u]] for u in range(2)]
        put_state(j, 0, own[0] * own_decay[1] + own[1], own_decay[0] * own_decay[1])
        state_copy(j, 0).start()

    def put_state(j, n, value, decay):
        states[j, n, pl.ds(0, HEAD), :] = value
        states[j, n, pl.ds(HEAD, 8), :] = jnp.broadcast_to(decay, (8, HEAD))

    def get_state(j, n):
        return states[j, n, pl.ds(0, HEAD), :], states[j, n, pl.ds(HEAD, 1), :]

    def along_pair(j):
        state_copy(j, 0).wait_recv()
        (own, own_decay), (mate, mate_decay) = get_state(j, 0), get_state(j, 1)
        after = odd == 1
        joined = jnp.where(after, mate * own_decay + own, own * mate_decay + mate)
        put_state(j, 2, joined, own_decay * mate_decay)
        state_copy(j, 1).start()

    def along_x(j):
        state_copy(j, 1).wait_recv()
        (mate, mate_decay), (own, own_decay), (pairs, pairs_decay) = get_state(j, 1), get_state(j, 2), get_state(j, 3)
        second, after = x >= 2, odd == 1
        total[j] = jnp.where(second, pairs * own_decay + own, own * pairs_decay + pairs)
        total_copy(j).start()
        near, near_decay = jnp.where(after, mate, 0.0), jnp.where(after, mate_decay, 1.0)
        put_state(j, 4, near + jnp.where(second, pairs * near_decay, 0.0), jnp.where(second, pairs_decay * near_decay, near_decay))

    def score(j):
        all_queries, all_values = summed(0, j), summed(2, j)
        queries = [all_queries[rows] for rows in lanes]
        keys = [gates[j, rows, :] for rows in lanes]
        scores = [jnp.where(t == r, jnp.sum(queries[u] * keys[u], axis=1, keepdims=True), 0.0) for u in range(2)]
        differ = jnp.where(t > r, t ^ r, 0)
        for i, m in enumerate(LEVELS):
            upper = (t & m) != 0
            mask = (differ >> (len(LEVELS) - 1 - i)) == 1
            for u in range(2):
                item = halves(jnp.where(upper, queries[u], keys[u]) * decays[j, i, :, lanes[u]])
                scores[u] = jnp.where(mask, dot3(item, item, (1, 1)), scores[u])
        for u in range(2):
            outputs = dot3(halves(scores[u]), halves(all_values[lanes[u]]), (1, 0))
            decayed = queries[u] * decays[j, len(LEVELS), :, lanes[u]]
            if u == 1:
                outputs = outputs + dot3(halves(decayed), halves(first_state[j]), (1, 1))
                decayed = decayed * decays[j, len(LEVELS), pl.ds(TILE - 1, 1), lanes[0]]
            local_out[j, lanes[u], :] = outputs
            q_decayed[j, lanes[u], :] = decayed

    def finish(j):
        total_copy(j).wait_recv()
        row_state, row_decay = get_state(j, 4)
        incoming = row_state + jnp.where(yl == 1, from_pair[j] * row_decay, 0.0)
        outputs = local_out[j] + dot3(halves(q_decayed[j]), halves(incoming), (1, 1))
        mean_square = jnp.mean(outputs * outputs, axis=-1, keepdims=True)
        normed = (outputs * lax.rsqrt(mean_square + 1e-05) * affine[heads[j], pl.ds(1, 1), :]).astype(jnp.bfloat16)
        if j == 0:
            out[mine] = normed
        else:
            result[j] = normed
            result_copy(j).start()

    def drain():
        left_here(w_all.at[:, pl.ds(0, Z - 1), 0, pl.ds(0, 32)], w1_s)
        left_here(w_all.at[:, pl.ds(0, Z - 1), :, pl.ds(0, 240)], ag_s)
        left_here(w_all.at[:, 0, 0], e_s)
        left_here(t_all.at[:, :, pl.ds(0, 480)], t_s)
        left_here(acc.at[0, :, pl.ds(0, 3 * 512)], p_s)
        left_here(states.at[:, pl.ds(0, 2)], xs_s)
        left_here(total, ys_s)
        left_here(result.at[pl.ds(0, 3)], o_s)
        left_here(affine.at[pl.ds(0, 3)], f_s)

    def share_affine():
        affine[mine] = jnp.zeros((8, HEAD), jnp.float32)
        affine[mine, pl.ds(0, 1), :] = bias[...]
        affine[mine, pl.ds(1, 1), :] = gain[...]
        for n in range(3):
            affine_copy(n).start()

    def take_affine():
        arrived(affine.at[pl.ds(0, 3)], f_r)

    steps = {
        "cross_send": cross_send, "w_send": w_send, "own_send": own_send, "own_step": own_step, "ring": ring, "ready": ready, "project": project, "project_in_turn": project_in_turn, "collect": collect,
        "gate": gate, "levels": levels, "state": state, "along_pair": along_pair, "along_x": along_x, "score": score, "finish": finish, "drain": drain, "share_affine": share_affine, "take_affine": take_affine,
        "a": lambda u, n: spread_step(0, u, n), "b": lambda u, n: spread_step(1, u, n), "sums": make_sums,
    }
    own_tokens().start()
    for what, *which in SCHEDULE:
        with jax.named_scope(what):
            steps[what](*which)
    arrived(result.at[pl.ds(0, 3)], o_r)


def body(tokens, q_weight, forget_weight, value_weight, forget_bias, norm_gain):
    seqs = tokens.shape[0]
    dma = pltpu.SemaphoreType.DMA
    any_ = pl.BlockSpec(memory_space=pl.ANY)
    vmem = pl.BlockSpec(memory_space=pltpu.VMEM)
    units = len(UNITS)
    f32, bf16 = jnp.float32, jnp.bfloat16
    return pl.pallas_call(
        layer_kernel,
        out_shape=pltpu.VMEM((seqs, 256, HEAD), bf16),
        in_specs=[any_] * 4 + [vmem] * 2,
        out_specs=vmem,
        scratch_shapes=[
            pltpu.VMEM((3, Z, 2, 256, 512), bf16),
            pltpu.VMEM((2, Z, 512, 256), bf16),
            pltpu.VMEM((2, 256, 3 * 512), f32),
            pltpu.VMEM((256, 3 * 512), f32),
            pltpu.VMEM(((len(LEVELS) + 2) * TILE, 3 * TILE), bf16),
            pltpu.VMEM((HEADS_HERE, 3 * TILE, 2 * TILE), bf16),
            pltpu.VMEM((HEADS_HERE, len(LEVELS) + 2, TILE, 2 * TILE), f32),
            pltpu.VMEM((HEADS_HERE, 256, HEAD), f32),
            pltpu.VMEM((HEADS_HERE, HEAD, HEAD), f32),
            pltpu.VMEM((HEADS_HERE, 256, HEAD), f32),
            pltpu.VMEM((HEADS_HERE, 256, HEAD), f32),
            pltpu.VMEM((HEADS_HERE, 5, HEAD + 8, HEAD), f32),
            pltpu.VMEM((HEADS_HERE, HEAD, HEAD), f32),
            pltpu.VMEM((HEADS_HERE, HEAD, HEAD), f32),
            pltpu.VMEM((HEADS_HERE, 256, HEAD), bf16),
            pltpu.VMEM((HEADS_HERE, 8, HEAD), f32),
            dma, dma((units,)),
            dma, dma((units, 2)),
            dma, dma((units, 2)),
            dma, dma((units, 8)),
            dma((2,)), dma, dma((2, 2, 4)),
            dma, dma((len(PRODUCTS),)),
            dma, dma((HEADS_HERE, 2)),
            dma, dma((HEADS_HERE,)),
            dma, dma,
            dma, dma,
        ],
        compiler_params=pltpu.CompilerParams(collective_id=0, has_side_effects=True, vmem_limit_bytes=56 * 2**20),
        name="layer",
    )(tokens, q_weight, forget_weight, value_weight, forget_bias.reshape(1, HEAD), norm_gain.reshape(1, HEAD))


def solution(mesh):
    placed = (
        P(None, "ctx", "zero"),
        P("zero", None),
        P("zero", None),
        P("zero", None),
        P("zero"),
        P("zero"),
    )
    return jax.shard_map(
        body, mesh=mesh, in_specs=placed, out_specs=P(None, "ctx", "zero"), check_vma=False
    )
```

```python
import jax
import jax.numpy as jnp
from jax import lax
from jax.experimental import pallas as pl
from jax.experimental.pallas import tpu as pltpu
from jax.sharding import PartitionSpec as P

MESH = pl.DeviceIdType.MESH
HEAD = 128
TILE = 128
LEVELS = (64, 32, 16, 8, 4, 2, 1)
OFFSETS = (4, 3, 5, 1, 7, 2, 6, 0)
SLOT = {offset: i for i, offset in enumerate(OFFSETS)}
X, Y, Z = 4, 4, 8
HEADS_HERE = 4
UNITS = ((1, 0, 128), (1, 128, 128), (1, 256, 256), (2, 0, 256), (2, 256, 256), (0, 0, 256), (0, 256, 256))
Y_FIRST = (4, 4, 4, 3, 4, 3, 3)
PRODUCTS = ((1, 0, 512), (2, 0, 512), (0, 0, 512))
SCHEDULE = (
    ("cross_send",), ("w_send", 0, 1), ("share_affine",), ("w_send", 6, 1), ("w_send", 0, 0), ("own_send", 0),
    ("w_send", 1, 0), ("w_send", 3, 0), ("own_send", 5), ("b", 0, 0), ("w_send", 3, 1), ("w_send", 4, 1), ("w_send", 2, 0),
    ("b", 6, 0), ("a", 0, 0), ("a", 1, 0), ("b", 0, 1), ("w_send", 1, 1), ("a", 3, 0), ("b", 6, 1), ("own_step", 0),
    ("b", 3, 0), ("b", 0, 2), ("w_send", 2, 1), ("w_send", 4, 0), ("own_step", 5), ("b", 4, 0), ("a", 0, 1), ("a", 1, 1),
    ("a", 2, 0), ("a", 3, 1), ("w_send", 6, 0), ("b", 1, 0), ("ring", 0, 0, 0), ("ring", 0, 1, 0), ("ring", 1, 0, 0),
    ("ring", 1, 1, 0), ("b", 3, 1), ("b", 2, 0), ("w_send", 5, 0), ("b", 4, 1), ("b", 0, 3), ("a", 4, 0), ("b", 1, 1),
    ("a", 0, 2), ("own_send", 1), ("a", 1, 2), ("own_send", 2), ("a", 6, 0), ("b", 2, 1), ("a", 2, 1), ("b", 1, 2),
    ("ring", 0, 0, 1), ("a", 4, 1), ("own_step", 1), ("a", 0, 3), ("own_step", 2), ("ring", 0, 1, 1), ("a", 6, 1),
    ("a", 2, 2), ("a", 1, 3), ("a", 3, 2), ("b", 2, 2), ("own_send", 4), ("ring", 1, 0, 1), ("b", 1, 3), ("ready", 0),
    ("b", 3, 2), ("ring", 1, 1, 1), ("a", 5, 0), ("a", 2, 3), ("a", 4, 2), ("w_send", 5, 1), ("own_send", 6), ("b", 2, 3),
    ("own_send", 3), ("b", 4, 2), ("ring", 0, 0, 2), ("own_step", 4), ("ready", 1), ("ring", 0, 1, 2), ("a", 3, 3),
    ("ring", 1, 0, 2), ("b", 3, 3), ("a", 5, 1), ("ring", 1, 1, 2), ("b", 5, 0), ("own_step", 6), ("own_step", 3),
    ("ready", 2), ("take_affine",), ("project", 0, 3, 8), ("a", 4, 3), ("a", 6, 2), ("ring", 0, 0, 3), ("ring", 0, 1, 3),
    ("b", 4, 3), ("b", 6, 2), ("b", 5, 1), ("ring", 1, 0, 3), ("a", 5, 2), ("ready", 3), ("ring", 1, 1, 3), ("ready", 4),
    ("project", 1, 3, 8), ("a", 6, 3), ("b", 5, 2), ("ring", 0, 0, 4), ("ring", 1, 0, 4), ("ring", 0, 1, 4),
    ("ring", 1, 1, 4), ("project", 0, 0, 3), ("project", 1, 0, 3), ("b", 6, 3), ("a", 5, 3), ("collect", 0), ("gate", 2),
    ("gate", 3), ("gate", 1), ("collect", 1), ("state", 2), ("state", 3), ("state", 1), ("gate", 0), ("state", 0),
    ("levels", 2), ("levels", 3), ("levels", 1), ("levels", 0), ("b", 5, 3), ("along_pair", 2), ("along_pair", 3),
    ("along_pair", 1), ("along_x", 2), ("along_pair", 0), ("ready", 6), ("ready", 5), ("project_in_turn", 2), ("along_x", 3),
    ("along_x", 1), ("collect", 2), ("score", 2), ("along_x", 0), ("finish", 2), ("score", 3), ("finish", 3), ("score", 1),
    ("finish", 1), ("score", 0), ("finish", 0), ("drain",),
)


def coords():
    c, zi = lax.axis_index("ctx"), lax.axis_index("zero")
    return lax.rem(c, X), c // X, zi // 4, lax.rem(zi // 2, 2), lax.rem(zi, 2)


def place(x, yl, z, yh, k):
    return (yl * X + x, z * 4 + yh * 2 + k)


def wrap(value, n):
    return lax.rem(value + n, n)


def halves(value):
    high = value.astype(jnp.bfloat16)
    return high, (value - high.astype(jnp.float32)).astype(jnp.bfloat16)


def dot3(a, b, contract):
    (ah, al), (bh, bl) = a, b
    lhs = jnp.concatenate([ah, ah, al], axis=contract[0])
    rhs = jnp.concatenate([bh, bl, bh], axis=contract[1])
    return lax.dot_general(lhs, rhs, (((contract[0],), (contract[1],)), ((), ())), preferred_element_type=jnp.float32)


def log1p_unit(e):
    w = e / (2.0 + e)
    w2 = w * w
    series = jnp.full_like(w2, 1.0 / 17)
    for odd in (15, 13, 11, 9, 7, 5, 3, 1):
        series = series * w2 + 1.0 / odd
    return 2.0 * w * series


def layer_kernel(tok, wq, wf, wv, bias, gain, out, w_all, t_all, acc, other, sums, logs, decays, key_parts, gates, first_state, local_out, q_decayed,
                 states, total, from_pair, result, affine, own_s, last_r, e_s, e_r, w1_s, w1_r, ag_s, ag_r, y0_r, t_s, z_r, p_s, p_r,
                 xs_s, xs_r, ys_s, ys_r, o_s, o_r, f_s, f_r):
    x, yl, z, yh, k = coords()
    z_next, z_prev = wrap(z + 1, Z), wrap(z - 1, Z)
    x_next, x_prev = wrap(x + 1, X), wrap(x - 1, X)
    y = yh * 2 + yl
    y_next, y_prev = wrap(y + 1, Y), wrap(y - 1, Y)
    yh_next, yl_next, yh_prev, yl_prev = y_next // 2, lax.rem(y_next, 2), y_prev // 2, lax.rem(y_prev, 2)
    z_ways = (place(x, yl, z_next, yh, k), place(x, yl, z_prev, yh, k))
    x_ways = (place(x_next, yl, z, yh, k), place(x_prev, yl, z, yh, k))
    y_ways = (place(x, yl_next, z, yh_next, k), place(x, yl_prev, z, yh_prev, k))
    odd = lax.rem(x, 2)
    row = (place(x + 1 - 2 * odd, yl, z, yh, k), place(X - 1 - x, yl, z, yh, k))
    far = place(x, yl, z, 1 - yh, k)
    pair = place(x, 1 - yl, z, yh, k)
    opposite = place(x, 1 - yl, z, 1 - yh, k)
    sibling = place(x, yl, z, yh, 1 - k)
    diagonal = place(x, yl, z, 1 - yh, 1 - k)
    mine = yh * 2 + k
    heads = (mine, yh * 2 + 1 - k, (1 - yh) * 2 + k, (1 - yh) * 2 + 1 - k)
    owner_of = (None, sibling, far, diagonal)
    holders = [wrap(z - dz, Z) for dz in OFFSETS]
    owners = [place(x, yl, zt, yh, k) for zt in holders]
    part_a = pl.multiple_of((x * 2 + yl) * 32, 32)
    part_b = pl.multiple_of((yl * X + x) * 32, 32)

    barrier = pltpu.get_barrier_semaphore()
    peers = list(x_ways) + list(y_ways) + [far, sibling, diagonal] + [owners[i] for i in range(Z) if i != SLOT[0]]
    for peer in peers:
        pl.semaphore_signal(barrier, inc=1, device_id=peer, device_id_type=MESH)

    def remote(src, dst, ss, rs, target):
        return pltpu.make_async_remote_copy(src, dst, ss, rs, device_id=target, device_id_type=MESH)


    def own_tokens():
        return pltpu.make_async_copy(tok.at[pl.ds(2 * yh, 2)], t_all.at[:, SLOT[0], pl.ds(pl.multiple_of(yh * 256, 256), 256)], own_s)

    def cross(q):
        return remote(tok.at[2 * (1 - yh) + q], t_all.at[q, SLOT[0], pl.ds(pl.multiple_of(yh * 256, 256), 256)],
                      t_s, y0_r.at[q], far)

    def hops(q, way):
        return 4 if way == q else 3

    def ring_copy(q, n, way, h):
        sign = (-1, 1)[way]
        here, there = SLOT[sign * (h - 1) % Z], SLOT[sign * h % Z]
        rows = pl.ds(pl.multiple_of((1 - yh if n else yh) * 256, 256), 256)
        return remote(t_all.at[q, here, rows], t_all.at[q, there, rows], t_s, z_r.at[q, n, h - 1], z_ways[way])

    def source(u, z_to, rows):
        w, first, count = UNITS[u]
        return (wq, wf, wv)[w].at[rows, pl.ds(pl.multiple_of(z_to * 512 + first, 128), count)]

    def w1(u, i):
        w, first, count = UNITS[u]
        half = int(i >= Y_FIRST[u])
        rows = pl.ds((part_a, part_b)[half], 32)
        return remote(source(u, holders[i], rows), w_all.at[w, i, yh, rows, pl.ds(first, count)], w1_s, w1_r.at[u, half], owners[i])

    def own_rows(u):
        w, first, count = UNITS[u]
        return pltpu.make_async_copy(source(u, z, pl.ds(0, 256)), w_all.at[w, SLOT[0], yh, :, pl.ds(first, count)], last_r.at[u])

    def other_rows(u, step):
        w, first, count = UNITS[u]
        half = pl.ds(pl.multiple_of((yl if step else 1 - yl) * 128, 128), 128)
        dst = w_all.at[w, SLOT[0], 1 - yh if step else yh, half, pl.ds(first, count)]
        return remote(dst if step else source(u, z, half), dst, e_s, last_r.at[u] if step else e_r.at[u], pair if step else opposite)

    def spread(u, step, way):
        w, first, count = UNITS[u]
        forward = step % 2 == 1
        begin, end = (0, Y_FIRST[u]) if step < 4 else (Y_FIRST[u], Z - 1)
        if forward and count > 128:
            first, count = first + way * (count // 2), count // 2
        elif forward:
            middle = (begin + end + 1) // 2
            begin, end = (middle, end) if way else (begin, middle)
        slots, cols = pl.ds(begin, end - begin), pl.ds(first, count)
        yh_from, yl_from = ((yh_prev, yl_prev), (yh_next, yl_next))[way] if forward else (yh, yl)
        x_from = (x_prev, x_next)[way] if forward else x
        if step in (0, 1):
            highs, rows, ways = pl.ds(yh_from, 1), pl.ds(pl.multiple_of((x * 2 + yl_from) * 32, 32), 32), y_ways
        elif step in (2, 3):
            highs, rows, ways = pl.ds(0, 2), pl.ds(pl.multiple_of(x_from * 64, 64), 64), x_ways
        elif step in (4, 5):
            highs, rows, ways = pl.ds(yh, 1), pl.ds(pl.multiple_of((yl * X + x_from) * 32, 32), 32), x_ways
        else:
            highs, rows, ways = pl.ds(yh_from, 1), pl.ds(pl.multiple_of(yl_from * 128, 128), 128), y_ways
        piece = w_all.at[w, slots, highs, rows, cols]
        sem = last_r.at[u] if step % 4 == 3 else ag_r.at[u, step - step // 4]
        return remote(piece, piece, ag_s, sem, ways[way])

    def partial(p):
        w, first, count = PRODUCTS[p]
        cols = pl.ds(w * 512 + first, count)
        return remote(acc.at[1 - k, :, cols], other.at[:, cols], p_s, p_r.at[p], sibling)

    def state_copy(j, step):
        return remote(states.at[j, 2 * step], states.at[j, 2 * step + 1], xs_s, xs_r.at[j, step], row[step])

    def total_copy(j):
        return remote(total.at[j], from_pair.at[j], ys_s, ys_r.at[j], pair)

    def result_copy(j):
        return remote(result.at[j], out.at[mine], o_s, o_r, owner_of[j])

    def affine_copy(n):
        piece = affine.at[mine]
        return remote(piece, piece, f_s, f_r, owner_of[1 + n])

    def arrived(piece, sem):
        remote(piece, piece, t_s, sem, far).wait_recv()

    def left_here(piece, sem):
        remote(piece, piece, sem, y0_r.at[0], far).wait_send()


    def both(make, *which):
        for way in range(2):
            make(*which, way).start()

    def wait_both(u, step):
        w, first, count = UNITS[u]
        slots = Y_FIRST[u] if step < 4 else Z - 1 - Y_FIRST[u]
        rows = (32, 32, 128, 128, 32, 32, 128, 128)[step] * (1 if step % 2 else 2)
        arrived(w_all.at[w, pl.ds(0, slots), 0, pl.ds(0, rows), pl.ds(first, count)], ag_r.at[u, step - step // 4])

    def cross_send():
        for q in range(2):
            cross(q).start()

    def w_send(u, half):
        for i in range(Y_FIRST[u], Z - 1) if half else range(Y_FIRST[u]):
            w1(u, i).start()

    def own_send(u):
        other_rows(u, 0).start()
        own_rows(u).start()

    def own_step(u):
        other_rows(u, 0).wait_recv()
        other_rows(u, 1).start()

    def ring(q, n, h):
        if h == 0:
            if n:
                cross(q).wait_recv()
            elif q == 0:
                own_tokens().wait()
        else:
            ways = sum(h <= hops(q, way) for way in range(2))
            arrived(t_all.at[0, 0, pl.ds(0, 256 * ways)], z_r.at[q, n, h - 1])
        for way in range(2):
            if h < hops(q, way):
                ring_copy(q, n, way, h + 1).start()

    def spread_step(half, u, n):
        if n == 0:
            w, first, count = UNITS[u]
            slots = Z - 1 - Y_FIRST[u] if half else Y_FIRST[u]
            arrived(w_all.at[w, pl.ds(0, slots), 0, pl.ds(0, 32), pl.ds(first, count)], w1_r.at[u, half])
        else:
            wait_both(u, 4 * half + n - 1)
        both(spread, u, 4 * half + n)

    def ready(u):
        w, first, count = UNITS[u]
        arrived(w_all.at[w, pl.ds(0, 5), 0, :, pl.ds(first, count)], last_r.at[u])

    def project(p, begin, end):
        w, first, count = PRODUCTS[p]
        lhs = jnp.concatenate(
            [
                jnp.concatenate([t_all[q, i, pl.ds(high * 256, 256), :] for i in range(begin, end) for high in range(2)], axis=1)
                for q in range(2)
            ],
            axis=0,
        )
        rhs = w_all[w, pl.ds(begin, end - begin), :, :, pl.ds(first, count)].reshape((end - begin) * 512, count)
        product = jnp.dot(lhs, rhs, preferred_element_type=jnp.float32)
        cols = pl.ds(w * 512 + first, count)
        for q in range(2):
            rows = product[q * 256 : (q + 1) * 256]
            acc[q, :, cols] = rows if end == Z else acc[q, :, cols] + rows
        if begin == 0:
            partial(p).start()

    def project_in_turn(p):
        w, first, count = PRODUCTS[p]
        cols = pl.ds(w * 512 + first, count)
        rhs = w_all[w, :, :, :, pl.ds(first, count)].reshape(Z * 512, count)
        for q in (1 - k, k):
            lhs = jnp.concatenate([t_all[q, i, pl.ds(high * 256, 256), :] for i in range(Z) for high in range(2)], axis=1)
            acc[q, :, cols] = jnp.dot(lhs, rhs, preferred_element_type=jnp.float32)
            if q is not k:
                partial(p).start()

    def collect(p):
        partial(p).wait_recv()

    def summed(weight, head):
        cols = pl.ds(pl.multiple_of(weight * 512 + heads[head] * HEAD, HEAD), HEAD)
        return acc[k, :, cols] + other[:, cols]

    t = lax.broadcasted_iota(jnp.int32, (TILE, TILE), 0)
    r = lax.broadcasted_iota(jnp.int32, (TILE, TILE), 1)
    lanes = [slice(u * TILE, (u + 1) * TILE) for u in range(2)]

    def make_sums():
        for i, m in enumerate(LEVELS + (TILE, 0)):
            if m == TILE:
                ones = jnp.where(r <= t, 1.0, 0.0)
            elif m == 0:
                ones = jnp.where(r > t, 1.0, 0.0)
            else:
                start = t // m * m
                after = jnp.where(r >= start, 1.0, 0.0) * jnp.where(r <= t, 1.0, 0.0)
                before = jnp.where(r > t, 1.0, 0.0) * jnp.where(r < start + m, 1.0, 0.0)
                ones = jnp.where((t // m) % 2 == 1, after, before)
            for j in range(3):
                sums[pl.ds(i * TILE, TILE), pl.ds(j * TILE, TILE)] = ones.astype(jnp.bfloat16)

    def gate(j):
        logit = summed(1, j) + affine[heads[j], pl.ds(0, 1), :]
        e = jnp.exp(-jnp.abs(logit))
        log_forget = jnp.minimum(logit, 0.0) - log1p_unit(e)
        gates[j] = jnp.where(logit >= 0.0, e, 1.0) / (1.0 + e)
        wide = jnp.concatenate([log_forget[:TILE], log_forget[TILE:]], axis=1)
        high = wide.astype(jnp.bfloat16)
        rest = wide - high.astype(jnp.float32)
        mid = rest.astype(jnp.bfloat16)
        low = (rest - mid.astype(jnp.float32)).astype(jnp.bfloat16)
        logs[j] = jnp.concatenate([high, mid, low], axis=0)
        fill_decays(j, len(LEVELS), len(LEVELS) + 2)

    def fill_decays(j, begin, end):
        for i in range(begin, end):
            decays[j, i] = jnp.exp(jnp.dot(sums[pl.ds(i * TILE, TILE), :], logs[j], preferred_element_type=jnp.float32))

    def levels(j):
        fill_decays(j, 0, len(LEVELS))
        for i in range(len(LEVELS)):
            for u in range(2):
                high, low = halves(gates[j, lanes[u], :] * decays[j, i, :, lanes[u]])
                key_parts[j, i, u] = jnp.concatenate([high, low], axis=0)

    def state(j):
        values = summed(2, j)
        own = []
        for u in range(2):
            kept = gates[j, lanes[u], :] * decays[j, len(LEVELS) + 1, :, lanes[u]]
            own.append(dot3(halves(values[lanes[u]]), halves(kept), (0, 0)))
        first_state[j] = own[0]
        own_decay = [decays[j, len(LEVELS), pl.ds(TILE - 1, 1), lanes[u]] for u in range(2)]
        put_state(j, 0, own[0] * own_decay[1] + own[1], own_decay[0] * own_decay[1])
        state_copy(j, 0).start()

    def put_state(j, n, value, decay):
        states[j, n, pl.ds(0, HEAD), :] = value
        states[j, n, pl.ds(HEAD, 8), :] = jnp.broadcast_to(decay, (8, HEAD))

    def get_state(j, n):
        return states[j, n, pl.ds(0, HEAD), :], states[j, n, pl.ds(HEAD, 1), :]

    def along_pair(j):
        state_copy(j, 0).wait_recv()
        (own, own_decay), (mate, mate_decay) = get_state(j, 0), get_state(j, 1)
        after = odd == 1
        joined = jnp.where(after, mate * own_decay + own, own * mate_decay + mate)
        put_state(j, 2, joined, own_decay * mate_decay)
        state_copy(j, 1).start()

    def along_x(j):
        state_copy(j, 1).wait_recv()
        (mate, mate_decay), (own, own_decay), (pairs, pairs_decay) = get_state(j, 1), get_state(j, 2), get_state(j, 3)
        second, after = x >= 2, odd == 1
        total[j] = jnp.where(second, pairs * own_decay + own, own * pairs_decay + pairs)
        total_copy(j).start()
        near, near_decay = jnp.where(after, mate, 0.0), jnp.where(after, mate_decay, 1.0)
        put_state(j, 4, near + jnp.where(second, pairs * near_decay, 0.0), jnp.where(second, pairs_decay * near_decay, near_decay))

    def score(j):
        all_queries, all_values = summed(0, j), summed(2, j)
        queries = [all_queries[rows] for rows in lanes]
        keys = [gates[j, rows, :] for rows in lanes]
        scores = [jnp.where(t == r, jnp.sum(queries[u] * keys[u], axis=1, keepdims=True), 0.0) for u in range(2)]
        differ = jnp.where(t > r, t ^ r, 0)
        for i, m in enumerate(LEVELS):
            picked = [slice(n + m, n + 2 * m) for n in range(0, TILE, 2 * m)] if m >= 8 else [slice(0, TILE)]
            mask = (differ >> (len(LEVELS) - 1 - i)) == 1
            for u in range(2):
                level = decays[j, i, :, lanes[u]]
                high, low = halves(jnp.concatenate([queries[u][rows] * level[rows] for rows in picked], axis=0))
                both_parts = lax.dot_general(jnp.concatenate([high, low], axis=0), key_parts[j, i, u], (((1,), (1,)), ((), ())),
                                             preferred_element_type=jnp.float32)
                count = high.shape[0]
                product = both_parts[:count, :TILE] + (both_parts[:count, TILE:] + both_parts[count:, :TILE])
                pieces, begin = [], 0
                for n, rows in enumerate(picked):
                    size = rows.stop - rows.start
                    if m >= 8:
                        pieces.append(scores[u][rows.start - m : rows.start])
                    pieces.append(jnp.where(mask[rows], product[begin : begin + size], scores[u][rows]))
                    begin += size
                scores[u] = jnp.concatenate(pieces, axis=0)
        for u in range(2):
            outputs = dot3(halves(scores[u]), halves(all_values[lanes[u]]), (1, 0))
            decayed = queries[u] * decays[j, len(LEVELS), :, lanes[u]]
            if u == 1:
                outputs = outputs + dot3(halves(decayed), halves(first_state[j]), (1, 1))
                decayed = decayed * decays[j, len(LEVELS), pl.ds(TILE - 1, 1), lanes[0]]
            local_out[j, lanes[u], :] = outputs
            q_decayed[j, lanes[u], :] = decayed

    def finish(j):
        total_copy(j).wait_recv()
        row_state, row_decay = get_state(j, 4)
        incoming = row_state + jnp.where(yl == 1, from_pair[j] * row_decay, 0.0)
        outputs = local_out[j] + dot3(halves(q_decayed[j]), halves(incoming), (1, 1))
        mean_square = jnp.mean(outputs * outputs, axis=-1, keepdims=True)
        normed = (outputs * lax.rsqrt(mean_square + 1e-05) * affine[heads[j], pl.ds(1, 1), :]).astype(jnp.bfloat16)
        if j == 0:
            out[mine] = normed
        else:
            result[j] = normed
            result_copy(j).start()

    def drain():
        left_here(w_all.at[:, pl.ds(0, Z - 1), 0, pl.ds(0, 32)], w1_s)
        left_here(w_all.at[:, pl.ds(0, Z - 1), :, pl.ds(0, 240)], ag_s)
        left_here(w_all.at[:, 0, 0], e_s)
        left_here(t_all.at[:, :, pl.ds(0, 480)], t_s)
        left_here(acc.at[0, :, pl.ds(0, 3 * 512)], p_s)
        left_here(states.at[:, pl.ds(0, 2)], xs_s)
        left_here(total, ys_s)
        left_here(result.at[pl.ds(0, 3)], o_s)
        left_here(affine.at[pl.ds(0, 3)], f_s)

    def put_affine():
        affine[mine] = jnp.zeros((8, HEAD), jnp.float32)
        affine[mine, pl.ds(0, 1), :] = bias[...]
        affine[mine, pl.ds(1, 1), :] = gain[...]

    def share_affine():
        for n in range(3):
            affine_copy(n).start()

    def take_affine():
        arrived(affine.at[pl.ds(0, 3)], f_r)

    steps = {
        "cross_send": cross_send, "w_send": w_send, "own_send": own_send, "own_step": own_step, "ring": ring, "ready": ready, "project": project, "project_in_turn": project_in_turn, "collect": collect,
        "gate": gate, "levels": levels, "state": state, "along_pair": along_pair, "along_x": along_x, "score": score, "finish": finish, "drain": drain, "share_affine": share_affine, "take_affine": take_affine,
        "a": lambda u, n: spread_step(0, u, n), "b": lambda u, n: spread_step(1, u, n),
    }
    own_tokens().start()
    make_sums()
    put_affine()
    pl.semaphore_wait(barrier, len(peers))
    for what, *which in SCHEDULE:
        with jax.named_scope(what):
            steps[what](*which)
    arrived(result.at[pl.ds(0, 3)], o_r)


def body(tokens, q_weight, forget_weight, value_weight, forget_bias, norm_gain):
    seqs = tokens.shape[0]
    dma = pltpu.SemaphoreType.DMA
    any_ = pl.BlockSpec(memory_space=pl.ANY)
    vmem = pl.BlockSpec(memory_space=pltpu.VMEM)
    units = len(UNITS)
    f32, bf16 = jnp.float32, jnp.bfloat16
    return pl.pallas_call(
        layer_kernel,
        out_shape=pltpu.VMEM((seqs, 256, HEAD), bf16),
        in_specs=[any_] * 4 + [vmem] * 2,
        out_specs=vmem,
        scratch_shapes=[
            pltpu.VMEM((3, Z, 2, 256, 512), bf16),
            pltpu.VMEM((2, Z, 512, 256), bf16),
            pltpu.VMEM((2, 256, 3 * 512), f32),
            pltpu.VMEM((256, 3 * 512), f32),
            pltpu.VMEM(((len(LEVELS) + 2) * TILE, 3 * TILE), bf16),
            pltpu.VMEM((HEADS_HERE, 3 * TILE, 2 * TILE), bf16),
            pltpu.VMEM((HEADS_HERE, len(LEVELS) + 2, TILE, 2 * TILE), f32),
            pltpu.VMEM((HEADS_HERE, len(LEVELS), 2, 2 * TILE, TILE), bf16),
            pltpu.VMEM((HEADS_HERE, 256, HEAD), f32),
            pltpu.VMEM((HEADS_HERE, HEAD, HEAD), f32),
            pltpu.VMEM((HEADS_HERE, 256, HEAD), f32),
            pltpu.VMEM((HEADS_HERE, 256, HEAD), f32),
            pltpu.VMEM((HEADS_HERE, 5, HEAD + 8, HEAD), f32),
            pltpu.VMEM((HEADS_HERE, HEAD, HEAD), f32),
            pltpu.VMEM((HEADS_HERE, HEAD, HEAD), f32),
            pltpu.VMEM((HEADS_HERE, 256, HEAD), bf16),
            pltpu.VMEM((HEADS_HERE, 8, HEAD), f32),
            dma, dma((units,)),
            dma, dma((units,)),
            dma, dma((units, 2)),
            dma, dma((units, 6)),
            dma((2,)), dma, dma((2, 2, 4)),
            dma, dma((len(PRODUCTS),)),
            dma, dma((HEADS_HERE, 2)),
            dma, dma((HEADS_HERE,)),
            dma, dma,
            dma, dma,
        ],
        compiler_params=pltpu.CompilerParams(collective_id=0, has_side_effects=True, vmem_limit_bytes=56 * 2**20),
        name="layer",
    )(tokens, q_weight, forget_weight, value_weight, forget_bias.reshape(1, HEAD), norm_gain.reshape(1, HEAD))


def solution(mesh):
    placed = (
        P(None, "ctx", "zero"),
        P("zero", None),
        P("zero", None),
        P("zero", None),
        P("zero"),
        P("zero"),
    )
    return jax.shard_map(
        body, mesh=mesh, in_specs=placed, out_specs=P(None, "ctx", "zero"), check_vma=False
    )
```
